32 devices in a mesh: dp: 8 (over z, x), seq: 4 (over y, core).
Axes of the slice: x: 2, y: 2, z: 4, core: 2. Of those that a mesh axis runs over, the one named last changes fastest.
Arguments:
- queries: bfloat16 [8, 512, 768], P('dp', 'seq'), may hold values from -720 to 720
- key_rows: bfloat16 [8, 512, 768], P('dp', 'seq'), may hold values from -7 to 7
- value_rows: bfloat16 [8, 512, 768], P('dp', 'seq'), may hold values from -6 to 6
- conv_weight: bfloat16 [768, 3, 768], replicated, may hold values from -0.125 to 0.125
- output_gradient: bfloat16 [8, 512, 768], P('dp', 'seq'), may hold values from -6 to 6
Outputs:
- conv_out: bfloat16 [8, 512, 768], P('dp', 'seq')
- grad_queries: bfloat16 [8, 512, 768], P('dp', 'seq')
- grad_keys: bfloat16 [8, 512, 768], P('dp', 'seq')
- grad_values: bfloat16 [8, 512, 768], P('dp', 'seq')
- grad_weight: float32 [768, 3, 768], P('dp', None, 'seq')
The draws below stay inside these ranges and needn't reach their ends.
All inputs are finite; a program needn't handle non-finite values.
Results may differ from the reference program's by a relative error of at most 0.014.
Values may be sent and summed in bfloat16 or wider, within the bound.
A program may use at most 64 MiB of HBM per device.

```python
import math
import jax
import jax.numpy as jnp
from jax import lax

D = 768
HEADS = 4
HEAD_DIM = 192
CH = 768
TAPS = 3
DILATION_STEP = 32
SEQUENCE_LENGTH = 512
SEQS = 8


def drawn_draws(key):
    shape = (SEQS, SEQUENCE_LENGTH, D)
    query_base = jnp.clip(jax.random.normal(jax.random.fold_in(key, 11), shape, jnp.float32), -6.0, 6.0)
    key_base = jnp.clip(jax.random.normal(jax.random.fold_in(key, 12), shape, jnp.float32), -6.0, 6.0)
    return (query_base, key_base)


def draw_queries(key, part):
    return drawn_draws(key)[0].astype(jnp.bfloat16)


def draw_key_rows(key, part):
    return drawn_draws(key)[1].astype(jnp.bfloat16)


def with_spikes(drawn, rng, source, target, blocks, factor):
    owner, partner = [(jnp.arange(drawn.shape[axis_at]) // (drawn.shape[axis_at] // blocks)).reshape([-1 if axis == axis_at else 1 for axis in range(drawn.ndim)]) for axis_at in (source, target)]
    chosen = jax.random.permutation(rng, blocks)[partner]
    strong = (owner == chosen) | (owner == (partner + blocks // 2) % blocks)
    return jnp.where(strong, factor * drawn, drawn)


def block_scale(stream_key, dims, cuts, least, high):
    level, own = 1.0, jax.random.fold_in(stream_key, 6)
    for dim, parts in cuts:
        draws = jnp.exp(jax.random.uniform(jax.random.fold_in(own, dim), (parts,), jnp.float32, least / len(cuts), high / len(cuts)))
        level = level * jnp.repeat(draws, dims[dim] // parts).reshape([-1 if axis == dim else 1 for axis in range(len(dims))])
    return level


def centred(rng, shape, scale, bound, cuts=(), held_as=jnp.bfloat16):
    entries = scale * jax.random.normal(rng, shape, jnp.float32)
    if cuts:
        entries = entries * block_scale(rng, shape, cuts, -0.22, 0.18)
    return jnp.clip(entries, -bound, bound).astype(held_as)


def heavy_noise(stream_key, extent, deviation, limit, cuts, heavy, dtype=jnp.bfloat16):
    values = deviation * jax.random.normal(stream_key, extent, jnp.float32)
    if cuts:
        values = values * block_scale(stream_key, extent, cuts, -0.22, 0.18)
    return jnp.clip(with_spikes(values, jax.random.fold_in(stream_key, 3), *heavy), -limit, limit).astype(dtype)


def setup_inputs(seed: int = 0) -> dict:
    key_list = jax.random.split(jax.random.key(seed), 6)
    queries = draw_queries(jax.random.fold_in(key_list[5], 71), 0)
    key_rows = draw_key_rows(jax.random.fold_in(key_list[5], 71), 0)
    value_rows = centred(key_list[2], (SEQS, SEQUENCE_LENGTH, D), 1.0, 6.0, ((0, 8), (1, 4)))
    conv_weight = centred(key_list[3], (D, TAPS, CH), (TAPS * D) ** -0.5, 0.125)
    output_gradient = heavy_noise(key_list[4], (SEQS, SEQUENCE_LENGTH, CH), 1.0, 6.0, ((0, 8), (1, 4)), (0, 2, 8, 2.0))
    return {"queries": queries, "key_rows": key_rows, "value_rows": value_rows, "conv_weight": conv_weight, "output_gradient": output_gradient}


tanh_scale = 0.7978845608028654
cubic_term = 0.044715
norm_epsilon = 1e-06

def gelu_pair(value):
    inner = tanh_scale * (value + cubic_term * value * value * value)
    tangent = jnp.tanh(inner)
    result = 0.5 * value * (1.0 + tangent)
    slope = 0.5 * (1.0 + tangent) + 0.5 * value * (1.0 - tangent * tangent) * tanh_scale * (1.0 + 3.0 * cubic_term * value * value)
    return (result, slope)

def reference(queries, key_rows, value_rows, conv_weight, output_gradient):
    inverse = 1.0 / math.sqrt(HEAD_DIM)
    grad_scale = 1.0 / math.sqrt(SEQS * SEQUENCE_LENGTH)

    def per_sequence(running_sum, inputs):
        query, keys, values, incoming_gradient = inputs
        query_heads = query.astype(jnp.float32).reshape(SEQUENCE_LENGTH, HEADS, HEAD_DIM)
        key_heads = keys.astype(jnp.float32).reshape(SEQUENCE_LENGTH, HEADS, HEAD_DIM)
        value_heads = values.astype(jnp.float32).reshape(SEQUENCE_LENGTH, HEADS, HEAD_DIM)
        scores = jnp.einsum('qhd,khd->hqk', query_heads, key_heads) * inverse
        soft_exact = jax.nn.softmax(scores, axis=-1)
        soft_rounded = lax.optimization_barrier(soft_exact.astype(jnp.bfloat16)).astype(jnp.float32)
        attended = jnp.einsum('hqk,khd->qhd', soft_rounded, value_heads).reshape(SEQUENCE_LENGTH, D).astype(jnp.bfloat16)
        att_full = attended.astype(jnp.float32)
        mean_square = lax.optimization_barrier(jnp.mean(att_full * att_full, axis=-1, keepdims=True))
        norm_factor = lax.rsqrt(mean_square + norm_epsilon)
        normed = att_full * norm_factor
        gelu_value, gelu_slope = gelu_pair(normed)
        activation_output = gelu_value.astype(jnp.bfloat16)
        padded_input = jnp.pad(activation_output, ((DILATION_STEP, DILATION_STEP), (0, 0)))
        padded_gradient = jnp.pad(incoming_gradient, ((DILATION_STEP, DILATION_STEP), (0, 0)))
        conv_sum = jnp.zeros((SEQUENCE_LENGTH, CH), jnp.float32)
        grad_acted = jnp.zeros((SEQUENCE_LENGTH, D), jnp.float32)
        tap_terms = []
        for kernel_tap_index in range(TAPS):
            shifted_input = padded_input[kernel_tap_index * DILATION_STEP:kernel_tap_index * DILATION_STEP + SEQUENCE_LENGTH]
            conv_sum = conv_sum + jnp.dot(shifted_input, conv_weight[:, kernel_tap_index, :], preferred_element_type=jnp.float32)
            reverse_rows = padded_gradient[(2 - kernel_tap_index) * DILATION_STEP:(2 - kernel_tap_index) * DILATION_STEP + SEQUENCE_LENGTH]
            grad_acted = grad_acted + jnp.dot(reverse_rows, conv_weight[:, kernel_tap_index, :].T, preferred_element_type=jnp.float32)
            tap_terms.append(jnp.dot(shifted_input.T, incoming_gradient, preferred_element_type=jnp.float32))
        local_term = jnp.stack(tap_terms, axis=1)
        conv_out = conv_sum.astype(jnp.bfloat16)
        grad_normed = grad_acted * gelu_slope
        mean_inner = lax.optimization_barrier(jnp.mean(grad_normed * normed, axis=-1, keepdims=True))
        grad_attended = (norm_factor * (grad_normed - normed * mean_inner)).astype(jnp.bfloat16)
        grad_heads = grad_attended.astype(jnp.float32).reshape(SEQUENCE_LENGTH, HEADS, HEAD_DIM)
        grad_values = jnp.einsum('hqk,qhd->khd', soft_rounded, grad_heads).reshape(SEQUENCE_LENGTH, D)
        grad_soft = jnp.einsum('qhd,khd->hqk', grad_heads, value_heads)
        row_inner = lax.optimization_barrier(jnp.sum(grad_soft * soft_exact, axis=-1, keepdims=True))
        grad_scores = lax.optimization_barrier((soft_exact * (grad_soft - row_inner) * inverse).astype(jnp.bfloat16)).astype(jnp.float32)
        grad_queries = jnp.einsum('hqk,khd->qhd', grad_scores, key_heads).reshape(SEQUENCE_LENGTH, D)
        grad_keys = jnp.einsum('hqk,qhd->khd', grad_scores, query_heads).reshape(SEQUENCE_LENGTH, D)
        results = (conv_out, grad_queries.astype(jnp.bfloat16), grad_keys.astype(jnp.bfloat16), grad_values.astype(jnp.bfloat16))
        return (running_sum + local_term, results)
    initial = jnp.zeros((D, TAPS, CH), jnp.float32)
    total_term, stacked = lax.scan(per_sequence, initial, (queries, key_rows, value_rows, output_gradient))
    return (stacked[0], stacked[1], stacked[2], stacked[3], total_term * grad_scale)
```

```python
import functools
import math

import jax
import jax.numpy as jnp
from jax import lax
from jax.experimental import pallas as pl
from jax.experimental.pallas import tpu as pltpu
from jax.sharding import PartitionSpec as P

HEAD_DIM = 192
WIN = 256
TAPS = 3
STEP = 32
N = 4
F32 = jnp.float32
BF16 = jnp.bfloat16
MESH = pl.DeviceIdType.MESH

tanh_scale = 0.7978845608028654
cubic_term = 0.044715
norm_epsilon = 1e-06


def gelu_pair(value):
    square = value * value
    inner = tanh_scale * (value + cubic_term * value * square)
    tangent = jnp.tanh(inner)
    half = 0.5 * (1.0 + tangent)
    result = value * half
    slope = half + 0.5 * value * (1.0 - tangent * tangent) * tanh_scale * (
        1.0 + 3.0 * cubic_term * square
    )
    return (result, slope)


def window_start(head):
    return pl.multiple_of(384 * (head // 2) + 128 * (head % 2), 128)


def nt(a, b):
    return lax.dot_general(a, b, (((1,), (1,)), ((), ())), preferred_element_type=F32)


def tn(a, b):
    return lax.dot_general(a, b, (((0,), (0,)), ((), ())), preferred_element_type=F32)


def nn(a, b):
    return lax.dot_general(a, b, (((1,), (0,)), ((), ())), preferred_element_type=F32)


def merge(even, odd):
    return jnp.concatenate(
        [even[:, :128], even[:, 128:] + odd[:, :128], odd[:, 128:]], axis=1
    )


def as_row(column):
    wide = jnp.broadcast_to(column, (column.shape[0], 128))
    return wide.T[:8]


def as_column(row):
    return jnp.broadcast_to(row, (128, 128)).T


def kernel(
    q_ref, k_ref, v_ref, g_ref, w_hbm,
    conv_ref, dq_ref, dk_ref, dv_ref, gw_ref,
    w_ref, qkv, gh, ga, gab, gg, soft, att, normed, gn, act, stat, dqkv, land,
    w_sem, send_sem, recv_sem,
):
    me = lax.axis_index("seq")
    rows, feats = q_ref.shape
    total = rows * N
    inverse = 1.0 / math.sqrt(HEAD_DIM)
    half_lanes = pl.multiple_of(384 * (me // 2), 128)
    my_start = window_start(me)
    my_rows = pl.multiple_of(rows * me, rows)
    sends = []

    def peer_of(o):
        return lax.rem(me + o, N)

    def rdma(phase, o, src, dst, when=None):
        copy = pltpu.make_async_remote_copy(
            src_ref=src, dst_ref=dst,
            send_sem=send_sem.at[phase, o], recv_sem=recv_sem.at[phase, o],
            device_id={"seq": peer_of(o)}, device_id_type=MESH,
        )
        return copy

    loads = [pltpu.make_async_copy(w_hbm.at[t], w_ref.at[t], w_sem.at[t]) for t in range(TAPS)]
    for load in loads:
        load.start()

    barrier = pltpu.get_barrier_semaphore()
    for o in (1, 2, 3):
        pl.semaphore_signal(barrier, inc=1, device_id={"seq": peer_of(o)}, device_id_type=MESH)
    pl.semaphore_wait(barrier, 3)

    has_next, has_prev = me < N - 1, me > 0
    down = pltpu.make_async_remote_copy(
        src_ref=g_ref.at[pl.ds(rows - STEP, STEP)], dst_ref=gh.at[pl.ds(0, STEP)],
        send_sem=send_sem.at[0, 0], recv_sem=recv_sem.at[0, 0],
        device_id={"seq": lax.rem(me + 1, N)}, device_id_type=MESH,
    )
    up = pltpu.make_async_remote_copy(
        src_ref=g_ref.at[pl.ds(0, STEP)], dst_ref=gh.at[pl.ds(rows + STEP, STEP)],
        send_sem=send_sem.at[1, 0], recv_sem=recv_sem.at[1, 0],
        device_id={"seq": lax.rem(me + N - 1, N)}, device_id_type=MESH,
    )
    pl.when(has_next)(lambda: down.start())
    pl.when(has_prev)(lambda: up.start())

    first = []
    for o in (2, 3, 1):
        start = window_start(peer_of(o))
        for i, ref in enumerate((q_ref, k_ref, v_ref)):
            copy = rdma(i, o, ref.at[:, pl.ds(start, WIN)], qkv.at[i, pl.ds(my_rows, rows)])
            copy.start()
            first.append(copy)
    grads = []
    for o in (2, 3, 1):
        lanes = pl.multiple_of(384 * (peer_of(o) // 2), 128)
        copy = rdma(
            3, o, g_ref.at[:, pl.ds(lanes, 384)],
            gg.at[pl.ds(pl.multiple_of(STEP + rows * me, STEP), rows)],
        )
        copy.start()
        grads.append(copy)

    for i, ref in enumerate((q_ref, k_ref, v_ref)):
        qkv[i, pl.ds(my_rows, rows)] = ref[:, pl.ds(my_start, WIN)]
    gg[pl.ds(0, STEP)] = jnp.zeros((STEP, 384), BF16)
    gg[pl.ds(STEP + total, STEP)] = jnp.zeros((STEP, 384), BF16)
    gg[pl.ds(pl.multiple_of(STEP + rows * me, STEP), rows)] = g_ref[:, pl.ds(half_lanes, 384)]
    gh[pl.ds(STEP, rows)] = g_ref[...]

    @pl.when(me == 0)
    def _():
        gh[pl.ds(0, STEP)] = jnp.zeros((STEP, feats), BF16)

    @pl.when(me == N - 1)
    def _():
        gh[pl.ds(rows + STEP, STEP)] = jnp.zeros((STEP, feats), BF16)

    pl.when(has_prev)(lambda: down.wait_recv())
    pl.when(has_next)(lambda: up.wait_recv())
    for load in loads:
        load.wait()

    acc = nt(gh[pl.ds(2 * STEP, rows)], w_ref[0])
    acc += nt(gh[pl.ds(STEP, rows)], w_ref[1])
    acc += nt(gh[pl.ds(0, rows)], w_ref[2])
    ga[...] = acc.astype(BF16)
    spread = []
    for o in (2, 3, 1):
        copy = rdma(
            4, o, ga.at[:, pl.ds(window_start(peer_of(o)), WIN)], gab.at[pl.ds(my_rows, rows)]
        )
        copy.start()
        spread.append(copy)
    gab[pl.ds(my_rows, rows)] = ga[:, pl.ds(my_start, WIN)]

    lane = lax.broadcasted_iota(jnp.int32, (rows, WIN), 1)
    low = 64 * (me % 2)
    mask32 = jnp.logical_and(lane >= low, lane < low + HEAD_DIM).astype(F32)
    mask = mask32.astype(BF16)

    for copy in first:
        copy.wait_recv()
    for i in range(3):
        for b in range(N):
            part = pl.ds(b * rows, rows)
            qkv[i, part] = qkv[i, part] * mask

    keys, values = qkv[1], qkv[2]
    for b in range(N):
        part = pl.ds(b * rows, rows)
        scores = nt(qkv[0, part], keys)
        top = jnp.max(scores, axis=-1, keepdims=True)
        expo = jnp.exp((scores - top) * inverse)
        prob = expo * (1.0 / jnp.sum(expo, axis=-1, keepdims=True))
        soft[part] = prob
        out = nn(prob.astype(BF16), values).astype(BF16)
        att[part] = out
        wide = out.astype(F32)
        stat[0, me, :, b * rows : (b + 1) * rows] = as_row(
            jnp.sum(wide * wide, axis=-1, keepdims=True)
        )
    stats = []
    for o in (2, 3, 1):
        copy = rdma(5, o, stat.at[0, me], stat.at[0, me])
        copy.start()
        stats.append(copy)
    for copy in spread:
        copy.wait_recv()
    for copy in stats:
        copy.wait_recv()

    act[me, pl.ds(0, STEP)] = jnp.zeros((STEP, WIN), BF16)
    act[me, pl.ds(STEP + total, STEP)] = jnp.zeros((STEP, WIN), BF16)

    def factor(b):
        lanes = slice(b * rows, (b + 1) * rows)
        mean = (
            stat[0, 0, :1, lanes] + stat[0, 1, :1, lanes]
            + stat[0, 2, :1, lanes] + stat[0, 3, :1, lanes]
        ) * (1.0 / feats)
        one = as_column(lax.rsqrt(mean + norm_epsilon))
        return jnp.concatenate([one, one], axis=1)

    for b in range(N):
        part = pl.ds(b * rows, rows)
        x = att[part].astype(F32) * factor(b)
        value, slope = gelu_pair(x)
        act[me, pl.ds(STEP + b * rows, rows)] = value.astype(BF16)
        grad = gab[part].astype(F32) * slope * mask32
        normed[part] = x
        gn[part] = grad
        stat[1, me, :, b * rows : (b + 1) * rows] = as_row(
            jnp.sum(grad * x, axis=-1, keepdims=True)
        )
    inner = []
    for o in (2, 3, 1):
        copy = rdma(6, o, stat.at[1, me], stat.at[1, me])
        copy.start()
        inner.append(copy)

    acts = []
    for o in (2, 3, 1):
        peer = peer_of(o)
        some = pl.ds(pl.multiple_of(rows * peer, rows), rows + 2 * STEP)
        full = rdma(7, o, act.at[me], act.at[me])
        piece = rdma(7, o, act.at[me, some], act.at[me, some])
        needs = peer % 2 == me // 2
        pl.when(needs)(lambda full=full: full.start())
        pl.when(jnp.logical_not(needs))(lambda piece=piece: piece.start())
        acts.append((o, needs, full, piece))

    for copy in inner:
        copy.wait_recv()

    queries = qkv[0]
    for b in range(N):
        part = pl.ds(b * rows, rows)
        lanes = slice(b * rows, (b + 1) * rows)
        mean = (
            stat[1, 0, :1, lanes] + stat[1, 1, :1, lanes]
            + stat[1, 2, :1, lanes] + stat[1, 3, :1, lanes]
        ) * (1.0 / feats)
        one = as_column(mean)
        mean = jnp.concatenate([one, one], axis=1)
        grad = (factor(b) * (gn[part] - normed[part] * mean)).astype(BF16)
        att[part] = grad
        prob = soft[part]
        gs = nt(grad, values)
        row_inner = jnp.sum(gs * prob, axis=-1, keepdims=True)
        ds = (prob * (gs - row_inner) * inverse).astype(BF16)
        dqkv[0, part] = nn(ds, keys).astype(BF16)
        pieces = (tn(ds, queries[b * rows : (b + 1) * rows]), tn(prob.astype(BF16), grad))
        sums = pieces if b == 0 else (sums[0] + pieces[0], sums[1] + pieces[1])
    dqkv[1] = sums[0].astype(BF16)
    dqkv[2] = sums[1].astype(BF16)

    back = []
    for o in (2, 3, 1):
        there = pl.ds(pl.multiple_of(rows * peer_of(o), rows), rows)
        for i in range(3):
            copy = rdma(8 + i, o, dqkv.at[i, there], land.at[me, i])
            copy.start()
            back.append(copy)
    for i in range(3):
        land[me, i] = dqkv[i, pl.ds(my_rows, rows)]

    def act_wait_recv(o, method):
        source = lax.rem(me + N - o, N)
        some = pl.ds(my_rows, rows + 2 * STEP)
        full = rdma(7, o, act.at[source], act.at[source])
        piece = rdma(7, o, act.at[source, some], act.at[source, some])
        needs = me % 2 == source // 2
        pl.when(needs)(lambda: full.wait_recv())
        pl.when(jnp.logical_not(needs))(lambda: piece.wait_recv())

    for o in (2, 3, 1):
        act_wait_recv(o, None)
    for copy in grads:
        copy.wait_recv()

    pair = 2 * (me % 2)
    whole = pl.ds(STEP, total)
    mine = merge(act[pair, whole], act[pair + 1, whole])
    mine = mine.T
    scale = 1.0 / math.sqrt(total * lax.axis_size("dp"))
    for t in range(TAPS):
        term = nn(mine, gg[pl.ds((2 - t) * STEP, total)])
        gw_ref[t] = (term * scale).astype(gw_ref.dtype)

    near = pl.ds(my_rows, rows + 2 * STEP)
    nearby = jnp.concatenate(
        [merge(act[0, near], act[1, near]), merge(act[2, near], act[3, near])], axis=1
    )
    out = nn(nearby[:rows], w_ref[0])
    out += nn(nearby[STEP : STEP + rows], w_ref[1])
    out += nn(nearby[2 * STEP :], w_ref[2])
    conv_ref[...] = out.astype(BF16)

    for copy in back:
        copy.wait_recv()
    for i, ref in enumerate((dq_ref, dk_ref, dv_ref)):
        ref[...] = jnp.concatenate(
            [merge(land[0, i], land[1, i]), merge(land[2, i], land[3, i])], axis=1
        )

    pl.when(has_next)(lambda: down.wait_send())
    pl.when(has_prev)(lambda: up.wait_send())
    for copy in first + grads + spread + stats + inner + back:
        copy.wait_send()
    for o, needs, full, piece in acts:
        pl.when(needs)(lambda full=full: full.wait_send())
        pl.when(jnp.logical_not(needs))(lambda piece=piece: piece.wait_send())


def body(queries, key_rows, value_rows, conv_weight, output_gradient):
    rows, feats = queries.shape[1:]
    total = rows * N
    vmem = pl.BlockSpec(memory_space=pltpu.VMEM)
    anyspace = pl.BlockSpec(memory_space=pl.ANY)
    shape = jax.ShapeDtypeStruct
    conv, dq, dk, dv, gw = pl.pallas_call(
        kernel,
        out_shape=[shape((rows, feats), BF16)] * 4 + [shape((TAPS, 384, 384), F32)],
        in_specs=[vmem] * 4 + [anyspace],
        out_specs=[vmem] * 5,
        scratch_shapes=[
            pltpu.VMEM((TAPS, feats, feats), BF16),
            pltpu.VMEM((3, total, WIN), BF16),
            pltpu.VMEM((rows + 2 * STEP, feats), BF16),
            pltpu.VMEM((rows, feats), BF16),
            pltpu.VMEM((total, WIN), BF16),
            pltpu.VMEM((total + 2 * STEP, 384), BF16),
            pltpu.VMEM((total, total), F32),
            pltpu.VMEM((total, WIN), BF16),
            pltpu.VMEM((total, WIN), F32),
            pltpu.VMEM((total, WIN), F32),
            pltpu.VMEM((N, total + 2 * STEP, WIN), BF16),
            pltpu.VMEM((2, N, 8, total), F32),
            pltpu.VMEM((3, total, WIN), BF16),
            pltpu.VMEM((N, 3, rows, WIN), BF16),
            pltpu.SemaphoreType.DMA((TAPS,)),
            pltpu.SemaphoreType.DMA((11, N)),
            pltpu.SemaphoreType.DMA((11, N)),
        ],
        compiler_params=pltpu.CompilerParams(
            collective_id=0, has_side_effects=True, vmem_limit_bytes=48 * 1024 * 1024
        ),
    )(
        queries[0], key_rows[0], value_rows[0], output_gradient[0],
        jnp.transpose(conv_weight, (1, 0, 2)),
    )
    pieces = lax.all_to_all(
        gw.astype(BF16), "seq", split_axis=2, concat_axis=1, tiled=True,
        axis_index_groups=[[0, 1], [2, 3]],
    )
    grad_weight = lax.psum_scatter(pieces.astype(F32), "dp", scatter_dimension=1, tiled=True)
    grad_weight = jnp.transpose(grad_weight, (1, 0, 2))
    return (conv[None], dq[None], dk[None], dv[None], grad_weight)


def solution(mesh):
    row_spec = P("dp", "seq", None)
    return jax.shard_map(
        body,
        mesh=mesh,
        in_specs=(row_spec, row_spec, row_spec, P(), row_spec),
        out_specs=(row_spec, row_spec, row_spec, row_spec, P("dp", None, "seq")),
        check_vma=False,
    )
```

```python
import functools
import math

import jax
import jax.numpy as jnp
from jax import lax
from jax.experimental import pallas as pl
from jax.experimental.pallas import tpu as pltpu
from jax.sharding import PartitionSpec as P

HEAD_DIM = 192
WIN = 256
TAPS = 3
STEP = 32
N = 4
F32 = jnp.float32
BF16 = jnp.bfloat16
MESH = pl.DeviceIdType.MESH

tanh_scale = 0.7978845608028654
cubic_term = 0.044715
norm_epsilon = 1e-06


def gelu_pair(value):
    square = value * value
    inner = tanh_scale * (value + cubic_term * value * square)
    tangent = jnp.tanh(inner)
    half = 0.5 * (1.0 + tangent)
    result = value * half
    slope = half + 0.5 * value * (1.0 - tangent * tangent) * tanh_scale * (
        1.0 + 3.0 * cubic_term * square
    )
    return (result, slope)


def window_start(head):
    return pl.multiple_of(384 * (head // 2) + 128 * (head % 2), 128)


def nt(a, b):
    return lax.dot_general(a, b, (((1,), (1,)), ((), ())), preferred_element_type=F32)


def tn(a, b):
    return lax.dot_general(a, b, (((0,), (0,)), ((), ())), preferred_element_type=F32)


def nn(a, b):
    return lax.dot_general(a, b, (((1,), (0,)), ((), ())), preferred_element_type=F32)


def merge(even, odd):
    return jnp.concatenate(
        [even[:, :128], even[:, 128:] + odd[:, :128], odd[:, 128:]], axis=1
    )


def as_row(column):
    wide = jnp.broadcast_to(column, (column.shape[0], 128))
    return wide.T[:8]


def as_column(row):
    return jnp.broadcast_to(row, (128, 128)).T


def kernel(
    q_ref, k_ref, v_ref, g_ref, w_hbm,
    conv_ref, dq_ref, dk_ref, dv_ref, gw_ref,
    w_ref, qkv, gh, ga, gab, gg, soft, att, normed, gn, act, stat, dqkv, land,
    w_sem, send_sem, recv_sem, *tail,
):
    me = lax.axis_index("seq")
    rows, feats = q_ref.shape
    ring = lax.axis_index("dp")
    tx, tz, core = ring % 2, ring // 2, me % 2
    total = rows * N
    inverse = 1.0 / math.sqrt(HEAD_DIM)
    half_lanes = pl.multiple_of(384 * (me // 2), 128)
    my_start = window_start(me)
    my_rows = pl.multiple_of(rows * me, rows)
    sends = []

    def peer_of(o):
        return lax.rem(me + o, N)

    def rdma(phase, o, src, dst, when=None):
        copy = pltpu.make_async_remote_copy(
            src_ref=src, dst_ref=dst,
            send_sem=send_sem.at[phase, o], recv_sem=recv_sem.at[phase, o],
            device_id={"seq": peer_of(o)}, device_id_type=MESH,
        )
        return copy

    loads = [pltpu.make_async_copy(w_hbm.at[t], w_ref.at[t], w_sem.at[t]) for t in range(TAPS)]
    grad_rows = pl.ds(pl.multiple_of(STEP + rows * me, STEP), rows)
    g_loads = [
        pltpu.make_async_copy(g_ref, gh.at[pl.ds(STEP, rows)], w_sem.at[TAPS]),
        pltpu.make_async_copy(g_ref.at[:, pl.ds(half_lanes, 384)], gg.at[grad_rows], w_sem.at[TAPS + 1]),
    ]
    own = [
        pltpu.make_async_copy(
            ref.at[:, pl.ds(my_start, WIN)], qkv.at[i, pl.ds(my_rows, rows)], w_sem.at[TAPS + 2 + i]
        )
        for i, ref in enumerate((q_ref, k_ref, v_ref))
    ]
    for load in g_loads + loads + own:
        load.start()

    barrier = pltpu.get_barrier_semaphore()
    for o in (1, 2, 3):
        pl.semaphore_signal(barrier, inc=1, device_id={"seq": peer_of(o)}, device_id_type=MESH)
    if tail:
        for other in [ring + 1 - 2 * tx] + [2 * lax.rem(tz + o, 4) + tx for o in (1, 2, 3)]:
            pl.semaphore_signal(barrier, inc=1, device_id={"dp": other}, device_id_type=MESH)
    pl.semaphore_wait(barrier, 7 if tail else 3)

    has_next, has_prev = me < N - 1, me > 0
    down = pltpu.make_async_remote_copy(
        src_ref=g_ref.at[pl.ds(rows - STEP, STEP)], dst_ref=gh.at[pl.ds(0, STEP)],
        send_sem=send_sem.at[0, 0], recv_sem=recv_sem.at[0, 0],
        device_id={"seq": lax.rem(me + 1, N)}, device_id_type=MESH,
    )
    up = pltpu.make_async_remote_copy(
        src_ref=g_ref.at[pl.ds(0, STEP)], dst_ref=gh.at[pl.ds(rows + STEP, STEP)],
        send_sem=send_sem.at[1, 0], recv_sem=recv_sem.at[1, 0],
        device_id={"seq": lax.rem(me + N - 1, N)}, device_id_type=MESH,
    )
    pl.when(has_next)(lambda: down.start())
    pl.when(has_prev)(lambda: up.start())

    first = []
    for o in (2, 3, 1):
        start = window_start(peer_of(o))
        for i, ref in enumerate((q_ref, k_ref, v_ref)):
            copy = rdma(i, o, ref.at[:, pl.ds(start, WIN)], qkv.at[i, pl.ds(my_rows, rows)])
            copy.start()
            first.append(copy)
    grads = []
    for o in (2, 3, 1):
        lanes = pl.multiple_of(384 * (peer_of(o) // 2), 128)
        copy = rdma(
            3, o, g_ref.at[:, pl.ds(lanes, 384)], gg.at[grad_rows]
        )
        copy.start()
        grads.append(copy)

    gg[pl.ds(0, STEP)] = jnp.zeros((STEP, 384), BF16)
    gg[pl.ds(STEP + total, STEP)] = jnp.zeros((STEP, 384), BF16)

    @pl.when(me == 0)
    def _():
        gh[pl.ds(0, STEP)] = jnp.zeros((STEP, feats), BF16)

    @pl.when(me == N - 1)
    def _():
        gh[pl.ds(rows + STEP, STEP)] = jnp.zeros((STEP, feats), BF16)

    pl.when(has_prev)(lambda: down.wait_recv())
    pl.when(has_next)(lambda: up.wait_recv())
    for load in g_loads + loads:
        load.wait()

    acc = nt(gh[pl.ds(2 * STEP, rows)], w_ref[0])
    acc += nt(gh[pl.ds(STEP, rows)], w_ref[1])
    acc += nt(gh[pl.ds(0, rows)], w_ref[2])
    ga[...] = acc.astype(BF16)
    spread = []
    for o in (2, 3, 1):
        copy = rdma(
            4, o, ga.at[:, pl.ds(window_start(peer_of(o)), WIN)], gab.at[pl.ds(my_rows, rows)]
        )
        copy.start()
        spread.append(copy)
    gab[pl.ds(my_rows, rows)] = ga[:, pl.ds(my_start, WIN)]

    lane = lax.broadcasted_iota(jnp.int32, (rows, WIN), 1)
    low = 64 * (me % 2)
    mask32 = jnp.logical_and(lane >= low, lane < low + HEAD_DIM).astype(F32)
    mask = mask32.astype(BF16)

    for load in own:
        load.wait()
    for copy in first:
        copy.wait_recv()
    for i in range(3):
        for b in range(N):
            part = pl.ds(b * rows, rows)
            qkv[i, part] = qkv[i, part] * mask

    keys, values = qkv[1], qkv[2]
    for b in range(N):
        part = pl.ds(b * rows, rows)
        scores = nt(qkv[0, part], keys)
        top = jnp.max(scores, axis=-1, keepdims=True)
        expo = jnp.exp((scores - top) * inverse)
        prob = expo * (1.0 / jnp.sum(expo, axis=-1, keepdims=True))
        soft[part] = prob
        out = nn(prob.astype(BF16), values).astype(BF16)
        att[part] = out
        wide = out.astype(F32)
        stat[0, me, :, b * rows : (b + 1) * rows] = as_row(
            jnp.sum(wide * wide, axis=-1, keepdims=True)
        )
    stats = []
    for o in (2, 3, 1):
        copy = rdma(5, o, stat.at[0, me], stat.at[0, me])
        copy.start()
        stats.append(copy)
    for copy in spread:
        copy.wait_recv()
    for copy in stats:
        copy.wait_recv()

    act[me, pl.ds(0, STEP)] = jnp.zeros((STEP, WIN), BF16)
    act[me, pl.ds(STEP + total, STEP)] = jnp.zeros((STEP, WIN), BF16)

    def factor(b):
        lanes = slice(b * rows, (b + 1) * rows)
        mean = (
            stat[0, 0, :1, lanes] + stat[0, 1, :1, lanes]
            + stat[0, 2, :1, lanes] + stat[0, 3, :1, lanes]
        ) * (1.0 / feats)
        one = as_column(lax.rsqrt(mean + norm_epsilon))
        return jnp.concatenate([one, one], axis=1)

    for b in range(N):
        part = pl.ds(b * rows, rows)
        x = att[part].astype(F32) * factor(b)
        value, slope = gelu_pair(x)
        act[me, pl.ds(STEP + b * rows, rows)] = value.astype(BF16)
        grad = gab[part].astype(F32) * slope * mask32
        normed[part] = x
        gn[part] = grad
        stat[1, me, :, b * rows : (b + 1) * rows] = as_row(
            jnp.sum(grad * x, axis=-1, keepdims=True)
        )
    inner = []
    for o in (2, 3, 1):
        copy = rdma(6, o, stat.at[1, me], stat.at[1, me])
        copy.start()
        inner.append(copy)

    acts = []
    for o in (2, 3, 1):
        peer = peer_of(o)
        some = pl.ds(pl.multiple_of(rows * peer, rows), rows + 2 * STEP)
        full = rdma(7, o, act.at[me], act.at[me])
        piece = rdma(7, o, act.at[me, some], act.at[me, some])
        needs = peer % 2 == me // 2
        pl.when(needs)(lambda full=full: full.start())
        pl.when(jnp.logical_not(needs))(lambda piece=piece: piece.start())
        acts.append((o, needs, full, piece))

    for copy in inner:
        copy.wait_recv()

    queries = qkv[0]
    for b in range(N):
        part = pl.ds(b * rows, rows)
        lanes = slice(b * rows, (b + 1) * rows)
        mean = (
            stat[1, 0, :1, lanes] + stat[1, 1, :1, lanes]
            + stat[1, 2, :1, lanes] + stat[1, 3, :1, lanes]
        ) * (1.0 / feats)
        one = as_column(mean)
        mean = jnp.concatenate([one, one], axis=1)
        grad = (factor(b) * (gn[part] - normed[part] * mean)).astype(BF16)
        att[part] = grad
        prob = soft[part]
        gs = nt(grad, values)
        row_inner = jnp.sum(gs * prob, axis=-1, keepdims=True)
        ds = (prob * (gs - row_inner) * inverse).astype(BF16)
        dqkv[0, part] = nn(ds, keys).astype(BF16)
        pieces = (tn(ds, queries[b * rows : (b + 1) * rows]), tn(prob.astype(BF16), grad))
        sums = pieces if b == 0 else (sums[0] + pieces[0], sums[1] + pieces[1])
    dqkv[1] = sums[0].astype(BF16)
    dqkv[2] = sums[1].astype(BF16)

    back = []
    for o in (2, 3, 1):
        there = pl.ds(pl.multiple_of(rows * peer_of(o), rows), rows)
        for i in range(3):
            copy = rdma(8 + i, o, dqkv.at[i, there], land.at[me, i])
            copy.start()
            back.append(copy)
    for i in range(3):
        land[me, i] = dqkv[i, pl.ds(my_rows, rows)]

    def act_wait_recv(o, method):
        source = lax.rem(me + N - o, N)
        some = pl.ds(my_rows, rows + 2 * STEP)
        full = rdma(7, o, act.at[source], act.at[source])
        piece = rdma(7, o, act.at[source, some], act.at[source, some])
        needs = me % 2 == source // 2
        pl.when(needs)(lambda: full.wait_recv())
        pl.when(jnp.logical_not(needs))(lambda: piece.wait_recv())

    for o in (2, 3, 1):
        act_wait_recv(o, None)
    for copy in grads:
        copy.wait_recv()

    pair = 2 * (me % 2)
    whole = pl.ds(STEP, total)
    mine = merge(act[pair, whole], act[pair + 1, whole])
    mine = mine.T
    crossing = []
    scale = 1.0 / math.sqrt(total * lax.axis_size("dp"))
    for t in range(TAPS):
        term = nn(mine, gg[pl.ds((2 - t) * STEP, total)])
        term = term * scale
        if not tail:
            gw_ref[t] = term
            continue
        gwf, xs, xr, zs, zo, zr, fin, x_send, x_recv, z_send, z_recv, c_sem = tail
        gwf[t] = term
        xs[t] = term.astype(BF16)
        for j in range(2):
            there = pl.ds(pl.multiple_of(96 * (2 * j + 1 - tx), 96), 96)
            copy = pltpu.make_async_remote_copy(
                src_ref=xs.at[t, there], dst_ref=xr.at[t, j],
                send_sem=x_send.at[t, j], recv_sem=x_recv.at[t, j],
                device_id={"dp": ring + 1 - 2 * tx}, device_id_type=MESH,
            )
            copy.start()
            crossing.append(copy)

    near = pl.ds(my_rows, rows + 2 * STEP)
    nearby = jnp.concatenate(
        [merge(act[0, near], act[1, near]), merge(act[2, near], act[3, near])], axis=1
    )
    out = nn(nearby[:rows], w_ref[0])
    out += nn(nearby[STEP : STEP + rows], w_ref[1])
    out += nn(nearby[2 * STEP :], w_ref[2])
    conv_ref[...] = out.astype(BF16)

    along = []
    if tail:
        for t in range(TAPS):
            for j in range(2):
                crossing[2 * t + j].wait_recv()
                here = pl.ds(pl.multiple_of(96 * (2 * j + tx), 96), 96)
                block = gwf[t, here] + xr[t, j].astype(F32)
                zs[j, t] = block
                zo[j, t] = block.astype(BF16)
                target = 2 * core + j
                copy = pltpu.make_async_remote_copy(
                    src_ref=zo.at[j, t], dst_ref=zr.at[tz, t],
                    send_sem=z_send.at[t, j], recv_sem=z_recv.at[t, tz],
                    device_id={"dp": 2 * target + tx}, device_id_type=MESH,
                )
                pl.when(target != tz)(lambda copy=copy: copy.start())
                along.append((target != tz, copy))

    for copy in back:
        copy.wait_recv()
    for i, ref in enumerate((dq_ref, dk_ref, dv_ref)):
        ref[...] = jnp.concatenate(
            [merge(land[0, i], land[1, i]), merge(land[2, i], land[3, i])], axis=1
        )

    if tail:
        owner = tz // 2 == core
        other = 2 * (me // 2) + 1 - core
        lanes = pl.multiple_of(128 * (1 - core), 128)
        hand = [
            pltpu.make_async_remote_copy(
                src_ref=fin.at[t, :, pl.ds(lanes, WIN)], dst_ref=fin.at[t, :, pl.ds(lanes, WIN)],
                send_sem=c_sem.at[0, t], recv_sem=c_sem.at[1, t],
                device_id={"seq": other}, device_id_type=MESH,
            )
            for t in range(TAPS)
        ]
        mine_lanes = pl.multiple_of(128 * core, 128)
        take = [
            pltpu.make_async_remote_copy(
                src_ref=fin.at[t, :, pl.ds(mine_lanes, WIN)],
                dst_ref=fin.at[t, :, pl.ds(mine_lanes, WIN)],
                send_sem=c_sem.at[0, t], recv_sem=c_sem.at[1, t],
                device_id={"seq": other}, device_id_type=MESH,
            )
            for t in range(TAPS)
        ]

        @pl.when(owner)
        def _():
            for t in range(TAPS):
                fin[t] = zs[tz % 2, t]
                for o in (1, 2, 3):
                    source = lax.rem(tz + o, 4)
                    pltpu.make_async_remote_copy(
                        src_ref=zo.at[0, t], dst_ref=zr.at[source, t],
                        send_sem=z_send.at[t, 0], recv_sem=z_recv.at[t, source],
                        device_id={"dp": 2 * source + tx}, device_id_type=MESH,
                    ).wait_recv()
                    fin[t] += zr[source, t].astype(F32)
                hand[t].start()
            for copy in hand:
                copy.wait_send()

        @pl.when(jnp.logical_not(owner))
        def _():
            for copy in take:
                copy.wait_recv()

        for t in range(TAPS):
            both = fin[t, :, pl.ds(mine_lanes, WIN)]
            gw_ref[t] = jnp.where(core == 0, both[:, :HEAD_DIM], both[:, WIN - HEAD_DIM :])
        for go, copy in along:
            pl.when(go)(lambda copy=copy: copy.wait_send())

    pl.when(has_next)(lambda: down.wait_send())
    pl.when(has_prev)(lambda: up.wait_send())
    for copy in first + grads + spread + stats + inner + back + crossing:
        copy.wait_send()
    for o, needs, full, piece in acts:
        pl.when(needs)(lambda full=full: full.wait_send())
        pl.when(jnp.logical_not(needs))(lambda piece=piece: piece.wait_send())


def store_kernel(*refs):
    count = (len(refs) - 1) // 2
    copies = [
        pltpu.make_async_copy(refs[i], refs[count + i], refs[-1].at[i]) for i in range(count)
    ]
    for copy in copies:
        copy.start()
    for copy in copies:
        copy.wait()


def body(queries, key_rows, value_rows, conv_weight, output_gradient):
    rows, feats = queries.shape[1:]
    total = rows * N
    vmem = pl.BlockSpec(memory_space=pltpu.VMEM)
    anyspace = pl.BlockSpec(memory_space=pl.ANY)
    shape = jax.ShapeDtypeStruct
    inside = lax.axis_size("dp") == 8
    gw_shape = (TAPS, 96, HEAD_DIM) if inside else (TAPS, 384, 384)
    tail = [
        pltpu.VMEM((TAPS, 384, 384), F32),
        pltpu.VMEM((TAPS, 384, 384), BF16),
        pltpu.VMEM((TAPS, 2, 96, 384), BF16),
        pltpu.VMEM((2, TAPS, 96, 384), F32),
        pltpu.VMEM((2, TAPS, 96, 384), BF16),
        pltpu.VMEM((4, TAPS, 96, 384), BF16),
        pltpu.VMEM((TAPS, 96, 384), F32),
        pltpu.SemaphoreType.DMA((TAPS, 2)),
        pltpu.SemaphoreType.DMA((TAPS, 2)),
        pltpu.SemaphoreType.DMA((TAPS, 2)),
        pltpu.SemaphoreType.DMA((TAPS, 4)),
        pltpu.SemaphoreType.DMA((2, TAPS)),
    ]
    outs = pl.pallas_call(
        kernel,
        out_shape=[shape((rows, feats), BF16)] * 4 + [shape(gw_shape, F32)],
        in_specs=[pl.BlockSpec(memory_space=pltpu.HBM)] * 5,
        out_specs=[vmem] * 5,
        scratch_shapes=[
            pltpu.VMEM((TAPS, feats, feats), BF16),
            pltpu.VMEM((3, total, WIN), BF16),
            pltpu.VMEM((rows + 2 * STEP, feats), BF16),
            pltpu.VMEM((rows, feats), BF16),
            pltpu.VMEM((total, WIN), BF16),
            pltpu.VMEM((total + 2 * STEP, 384), BF16),
            pltpu.VMEM((total, total), F32),
            pltpu.VMEM((total, WIN), BF16),
            pltpu.VMEM((total, WIN), F32),
            pltpu.VMEM((total, WIN), F32),
            pltpu.VMEM((N, total + 2 * STEP, WIN), BF16),
            pltpu.VMEM((2, N, 8, total), F32),
            pltpu.VMEM((3, total, WIN), BF16),
            pltpu.VMEM((N, 3, rows, WIN), BF16),
            pltpu.SemaphoreType.DMA((TAPS + 5,)),
            pltpu.SemaphoreType.DMA((11, N)),
            pltpu.SemaphoreType.DMA((11, N)),
        ] + (tail if inside else []),
        compiler_params=pltpu.CompilerParams(
            collective_id=0, has_side_effects=True, vmem_limit_bytes=int(62.5 * 2**20)
        ),
    )(
        queries[0], key_rows[0], value_rows[0], output_gradient[0],
        jnp.transpose(conv_weight, (1, 0, 2)),
    )
    if not inside:
        pieces = lax.all_to_all(
            outs[4].astype(BF16), "seq", split_axis=2, concat_axis=1, tiled=True,
            axis_index_groups=[[0, 1], [2, 3]],
        )
        gw = lax.psum_scatter(pieces.astype(F32), "dp", scatter_dimension=1, tiled=True)
        outs = [*outs[:4], gw]
    else:
        outs = pl.pallas_call(
            store_kernel,
            out_shape=[shape(out.shape, out.dtype) for out in outs],
            in_specs=[anyspace] * 5,
            out_specs=[pl.BlockSpec(memory_space=pltpu.HBM)] * 5,
            scratch_shapes=[pltpu.SemaphoreType.DMA((5,))],
            compiler_params=pltpu.CompilerParams(vmem_limit_bytes=int(62.5 * 2**20)),
        )(*outs)
    return (*(out[None] for out in outs[:4]), jnp.transpose(outs[4], (1, 0, 2)))


def solution(mesh):
    row_spec = P("dp", "seq", None)
    return jax.shard_map(
        body,
        mesh=mesh,
        in_specs=(row_spec, row_spec, row_spec, P(), row_spec),
        out_specs=(row_spec, row_spec, row_spec, row_spec, P("dp", None, "seq")),
        check_vma=False,
    )
```

```python
import functools
import math

import jax
import jax.numpy as jnp
from jax import lax
from jax.experimental import pallas as pl
from jax.experimental.pallas import tpu as pltpu
from jax.sharding import PartitionSpec as P

HEAD_DIM = 192
WIN = 256
TAPS = 3
STEP = 32
N = 4
F32 = jnp.float32
BF16 = jnp.bfloat16
MESH = pl.DeviceIdType.MESH

tanh_scale = 0.7978845608028654
cubic_term = 0.044715
norm_epsilon = 1e-06


def gelu_pair(value):
    square = value * value
    inner = tanh_scale * (value + cubic_term * value * square)
    tangent = jnp.tanh(inner)
    half = 0.5 * (1.0 + tangent)
    result = value * half
    slope = half + 0.5 * value * (1.0 - tangent * tangent) * tanh_scale * (
        1.0 + 3.0 * cubic_term * square
    )
    return (result, slope)


def window_start(head):
    return pl.multiple_of(384 * (head // 2) + 128 * (head % 2), 128)


def nt(a, b):
    return lax.dot_general(a, b, (((1,), (1,)), ((), ())), preferred_element_type=F32)


def tn(a, b):
    return lax.dot_general(a, b, (((0,), (0,)), ((), ())), preferred_element_type=F32)


def nn(a, b):
    return lax.dot_general(a, b, (((1,), (0,)), ((), ())), preferred_element_type=F32)


def merge(even, odd):
    return jnp.concatenate(
        [even[:, :128], even[:, 128:] + odd[:, :128], odd[:, 128:]], axis=1
    )


def as_row(column):
    wide = jnp.broadcast_to(column, (column.shape[0], 128))
    return wide.T[:8]


def as_column(row):
    return jnp.broadcast_to(row, (128, 128)).T


def kernel(
    q_ref, k_ref, v_ref, g_ref, w_hbm,
    conv_ref, dq_ref, dk_ref, dv_ref, gw_ref,
    w_ref, qkv, gh, ga, gab, gg, soft, att, normed, gn, act, stat, dqkv, land,
    xq, xa, w_sem, send_sem, recv_sem, *tail,
):
    me = lax.axis_index("seq")
    rows, feats = q_ref.shape
    ring = lax.axis_index("dp")
    tx, tz, core = ring % 2, ring // 2, me % 2
    total = rows * N
    inverse = 1.0 / math.sqrt(HEAD_DIM)
    half_lanes = pl.multiple_of(384 * (me // 2), 128)
    my_start = window_start(me)
    my_rows = pl.multiple_of(rows * me, rows)
    sends = []

    chip = me // 2
    partner = 2 * chip + 1 - core
    cross = 2 * (1 - chip) + core
    diagonal = 2 * (1 - chip) + 1 - core
    cross_rows = pl.ds(pl.multiple_of(rows * cross, rows), rows)
    their_rows = pl.ds(pl.multiple_of(rows * partner, rows), rows)
    their_start = window_start(partner)
    across_lanes = pl.multiple_of(384 * (1 - chip), 128)
    mine_in_block = pl.ds(pl.multiple_of(128 * core, 128), WIN)
    theirs_in_block = pl.ds(pl.multiple_of(128 * (1 - core), 128), WIN)

    def peer_of(o):
        return (None, partner, cross, diagonal)[o]

    def rdma(phase, o, src, dst, target=None):
        copy = pltpu.make_async_remote_copy(
            src_ref=src, dst_ref=dst,
            send_sem=send_sem.at[phase, o], recv_sem=recv_sem.at[phase, o],
            device_id={"seq": peer_of(o) if target is None else target}, device_id_type=MESH,
        )
        return copy

    loads = [pltpu.make_async_copy(w_hbm.at[t], w_ref.at[t], w_sem.at[t]) for t in range(TAPS)]
    grad_rows = pl.ds(pl.multiple_of(STEP + rows * me, STEP), rows)
    g_loads = [
        pltpu.make_async_copy(g_ref, gh.at[pl.ds(STEP, rows)], w_sem.at[TAPS]),
        pltpu.make_async_copy(g_ref.at[:, pl.ds(half_lanes, 384)], gg.at[grad_rows], w_sem.at[TAPS + 1]),
    ]
    own = [
        pltpu.make_async_copy(
            ref.at[:, pl.ds(my_start, WIN)], qkv.at[i, pl.ds(my_rows, rows)], w_sem.at[TAPS + 2 + i]
        )
        for i, ref in enumerate((q_ref, k_ref, v_ref))
    ]
    for load in g_loads + loads + own:
        load.start()

    barrier = pltpu.get_barrier_semaphore()
    for o in (1, 2, 3):
        pl.semaphore_signal(barrier, inc=1, device_id={"seq": peer_of(o)}, device_id_type=MESH)
    if tail:
        for other in [ring + 1 - 2 * tx] + [2 * lax.rem(tz + o, 4) + tx for o in (1, 2, 3)]:
            pl.semaphore_signal(barrier, inc=1, device_id={"dp": other}, device_id_type=MESH)
    pl.semaphore_wait(barrier, 7 if tail else 3)

    has_next, has_prev = me < N - 1, me > 0
    down = pltpu.make_async_remote_copy(
        src_ref=g_ref.at[pl.ds(rows - STEP, STEP)], dst_ref=gh.at[pl.ds(0, STEP)],
        send_sem=send_sem.at[0, 0], recv_sem=recv_sem.at[0, 0],
        device_id={"seq": lax.rem(me + 1, N)}, device_id_type=MESH,
    )
    up = pltpu.make_async_remote_copy(
        src_ref=g_ref.at[pl.ds(0, STEP)], dst_ref=gh.at[pl.ds(rows + STEP, STEP)],
        send_sem=send_sem.at[1, 0], recv_sem=recv_sem.at[1, 0],
        device_id={"seq": lax.rem(me + N - 1, N)}, device_id_type=MESH,
    )
    pl.when(has_next)(lambda: down.start())
    pl.when(has_prev)(lambda: up.start())

    across, first, grads = [], [], []
    for i, ref in enumerate((q_ref, k_ref, v_ref)):
        copy = rdma(i, 2, ref.at[:, pl.ds(across_lanes, 384)], xq.at[i])
        copy.start()
        across.append(copy)
    for i, ref in enumerate((q_ref, k_ref, v_ref)):
        copy = rdma(i, 1, ref.at[:, pl.ds(their_start, WIN)], qkv.at[i, pl.ds(my_rows, rows)])
        copy.start()
        first.append(copy)
    g_across = rdma(3, 2, g_ref.at[:, pl.ds(across_lanes, 384)], gg.at[grad_rows])
    g_across.start()
    g_near = rdma(3, 1, g_ref.at[:, pl.ds(half_lanes, 384)], gg.at[grad_rows])
    g_near.start()
    grads = [g_across, g_near]

    gg[pl.ds(0, STEP)] = jnp.zeros((STEP, 384), BF16)
    gg[pl.ds(STEP + total, STEP)] = jnp.zeros((STEP, 384), BF16)

    @pl.when(me == 0)
    def _():
        gh[pl.ds(0, STEP)] = jnp.zeros((STEP, feats), BF16)

    @pl.when(me == N - 1)
    def _():
        gh[pl.ds(rows + STEP, STEP)] = jnp.zeros((STEP, feats), BF16)

    pl.when(has_prev)(lambda: down.wait_recv())
    pl.when(has_next)(lambda: up.wait_recv())
    for load in g_loads + loads:
        load.wait()

    acc = nt(gh[pl.ds(2 * STEP, rows)], w_ref[0])
    acc += nt(gh[pl.ds(STEP, rows)], w_ref[1])
    acc += nt(gh[pl.ds(0, rows)], w_ref[2])
    ga[...] = acc.astype(BF16)
    ga_across = rdma(4, 2, ga.at[:, pl.ds(across_lanes, 384)], xa)
    ga_across.start()
    ga_near = rdma(4, 1, ga.at[:, pl.ds(their_start, WIN)], gab.at[pl.ds(my_rows, rows)])
    ga_near.start()
    spread = [ga_across, ga_near]
    gab[pl.ds(my_rows, rows)] = ga[:, pl.ds(my_start, WIN)]

    lane = lax.broadcasted_iota(jnp.int32, (rows, WIN), 1)
    low = 64 * (me % 2)
    mask32 = jnp.logical_and(lane >= low, lane < low + HEAD_DIM).astype(F32)
    mask = mask32.astype(BF16)

    for i in range(3):
        across[i].wait_recv()
        copy = rdma(i, 3, xq.at[i, :, theirs_in_block], qkv.at[i, cross_rows], partner)
        copy.start()
        first.append(copy)
    for i in range(3):
        qkv[i, cross_rows] = xq[i, :, mine_in_block]
    for load in own:
        load.wait()
    for copy in first:
        copy.wait_recv()
    for i in range(3):
        for b in range(N):
            part = pl.ds(b * rows, rows)
            qkv[i, part] = qkv[i, part] * mask

    keys, values = qkv[1], qkv[2]
    for b in range(N):
        part = pl.ds(b * rows, rows)
        scores = nt(qkv[0, part], keys)
        top = jnp.max(scores, axis=-1, keepdims=True)
        expo = jnp.exp((scores - top) * inverse)
        prob = expo * (1.0 / jnp.sum(expo, axis=-1, keepdims=True))
        soft[part] = prob
        out = nn(prob.astype(BF16), values).astype(BF16)
        att[part] = out
        wide = out.astype(F32)
        stat[0, me, :, b * rows : (b + 1) * rows] = as_row(
            jnp.sum(wide * wide, axis=-1, keepdims=True)
        )
    stats = []
    for o in (2, 3, 1):
        copy = rdma(5, o, stat.at[0, me], stat.at[0, me])
        copy.start()
        stats.append(copy)
    ga_across.wait_recv()
    ga_hop = rdma(4, 3, xa.at[:, theirs_in_block], gab.at[cross_rows], partner)
    ga_hop.start()
    gab[cross_rows] = xa[:, mine_in_block]
    g_across.wait_recv()
    g_cross = pl.ds(pl.multiple_of(STEP + rows * cross, STEP), rows)
    g_hop = rdma(3, 3, gg.at[g_cross], gg.at[g_cross], partner)
    g_hop.start()
    spread.append(ga_hop)
    grads.append(g_hop)
    ga_near.wait_recv()
    ga_hop.wait_recv()
    for copy in stats:
        copy.wait_recv()

    act[me, pl.ds(0, STEP)] = jnp.zeros((STEP, WIN), BF16)
    act[me, pl.ds(STEP + total, STEP)] = jnp.zeros((STEP, WIN), BF16)

    def factor(b):
        lanes = slice(b * rows, (b + 1) * rows)
        mean = (
            stat[0, 0, :1, lanes] + stat[0, 1, :1, lanes]
            + stat[0, 2, :1, lanes] + stat[0, 3, :1, lanes]
        ) * (1.0 / feats)
        one = as_column(lax.rsqrt(mean + norm_epsilon))
        return jnp.concatenate([one, one], axis=1)

    for b in range(N):
        part = pl.ds(b * rows, rows)
        x = att[part].astype(F32) * factor(b)
        value, slope = gelu_pair(x)
        act[me, pl.ds(STEP + b * rows, rows)] = value.astype(BF16)
        grad = gab[part].astype(F32) * slope * mask32
        normed[part] = x
        gn[part] = grad
        stat[1, me, :, b * rows : (b + 1) * rows] = as_row(
            jnp.sum(grad * x, axis=-1, keepdims=True)
        )
    inner = []
    for o in (2, 3, 1):
        copy = rdma(6, o, stat.at[1, me], stat.at[1, me])
        copy.start()
        inner.append(copy)

    inside = pl.ds(STEP, total)
    forms = core == 1 - chip
    act_across = pltpu.make_async_remote_copy(
        src_ref=act.at[me, inside], dst_ref=act.at[me, inside],
        send_sem=send_sem.at[7, 0], recv_sem=recv_sem.at[7, core],
        device_id={"seq": 2 * (1 - chip) + chip}, device_id_type=MESH,
    )
    act_across.start()
    act_near = rdma(11, 1, act.at[me], act.at[me])
    act_near.start()

    @pl.when(forms)
    def _():
        for i in range(2):
            act[2 * (1 - chip) + i, pl.ds(0, STEP)] = jnp.zeros((STEP, WIN), BF16)
            act[2 * (1 - chip) + i, pl.ds(STEP + total, STEP)] = jnp.zeros((STEP, WIN), BF16)

    for copy in inner:
        copy.wait_recv()

    queries = qkv[0]
    for b in range(N):
        part = pl.ds(b * rows, rows)
        lanes = slice(b * rows, (b + 1) * rows)
        mean = (
            stat[1, 0, :1, lanes] + stat[1, 1, :1, lanes]
            + stat[1, 2, :1, lanes] + stat[1, 3, :1, lanes]
        ) * (1.0 / feats)
        one = as_column(mean)
        mean = jnp.concatenate([one, one], axis=1)
        grad = (factor(b) * (gn[part] - normed[part] * mean)).astype(BF16)
        att[part] = grad
        prob = soft[part]
        gs = nt(grad, values)
        row_inner = jnp.sum(gs * prob, axis=-1, keepdims=True)
        ds = (prob * (gs - row_inner) * inverse).astype(BF16)
        dqkv[0, part] = nn(ds, keys).astype(BF16)
        pieces = (tn(ds, queries[b * rows : (b + 1) * rows]), tn(prob.astype(BF16), grad))
        sums = pieces if b == 0 else (sums[0] + pieces[0], sums[1] + pieces[1])
    dqkv[1] = sums[0].astype(BF16)
    dqkv[2] = sums[1].astype(BF16)

    back = []
    for o in (2, 3, 1):
        there = pl.ds(pl.multiple_of(rows * peer_of(o), rows), rows)
        for i in range(3):
            copy = rdma(8 + i, o, dqkv.at[i, there], land.at[me, i])
            copy.start()
            back.append(copy)
    for i in range(3):
        land[me, i] = dqkv[i, pl.ds(my_rows, rows)]

    act_near.wait_recv()

    def act_hop(i, row):
        slot = 2 * (1 - chip) + i
        some = pl.ds(pl.multiple_of(rows * row, rows), rows + 2 * STEP)
        return rdma(12, i, act.at[slot, some], act.at[slot, some], partner)

    @pl.when(forms)
    def _():
        for i in range(2):
            slot = 2 * (1 - chip) + i
            pltpu.make_async_remote_copy(
                src_ref=act.at[slot, inside], dst_ref=act.at[slot, inside],
                send_sem=send_sem.at[7, 0], recv_sem=recv_sem.at[7, i],
                device_id={"seq": partner}, device_id_type=MESH,
            ).wait_recv()
            act_hop(i, partner).start()

    @pl.when(jnp.logical_not(forms))
    def _():
        for i in range(2):
            act_hop(i, me).wait_recv()

    for copy in (g_near, g_hop):
        copy.wait_recv()

    pair = 2 * core
    whole = pl.ds(STEP, total)
    mine = merge(act[pair, whole], act[pair + 1, whole])
    mine = mine.T
    crossing = []
    scale = 1.0 / math.sqrt(total * lax.axis_size("dp"))
    for t in range(TAPS):
        term = nn(mine, gg[pl.ds((2 - t) * STEP, total)])
        term = term * scale
        if not tail:
            gw_ref[t] = term
            continue
        gwf, xs, xr, zs, zo, zr, fin, x_send, x_recv, z_send, z_recv, c_sem = tail
        gwf[t] = term
        xs[t] = term.astype(BF16)
        for j in range(2):
            there = pl.ds(pl.multiple_of(96 * (2 * j + 1 - tx), 96), 96)
            copy = pltpu.make_async_remote_copy(
                src_ref=xs.at[t, there], dst_ref=xr.at[t, j],
                send_sem=x_send.at[t, j], recv_sem=x_recv.at[t, j],
                device_id={"dp": ring + 1 - 2 * tx}, device_id_type=MESH,
            )
            copy.start()
            crossing.append(copy)

    near = pl.ds(my_rows, rows + 2 * STEP)
    nearby = jnp.concatenate(
        [merge(act[0, near], act[1, near]), merge(act[2, near], act[3, near])], axis=1
    )
    out = nn(nearby[:rows], w_ref[0])
    out += nn(nearby[STEP : STEP + rows], w_ref[1])
    out += nn(nearby[2 * STEP :], w_ref[2])
    conv_ref[...] = out.astype(BF16)

    along = []
    if tail:
        for t in range(TAPS):
            for j in range(2):
                crossing[2 * t + j].wait_recv()
                here = pl.ds(pl.multiple_of(96 * (2 * j + tx), 96), 96)
                block = gwf[t, here] + xr[t, j].astype(F32)
                zs[j, t] = block
                zo[j, t] = block.astype(BF16)
                target = 2 * core + j
                copy = pltpu.make_async_remote_copy(
                    src_ref=zo.at[j, t], dst_ref=zr.at[tz, t],
                    send_sem=z_send.at[t, j], recv_sem=z_recv.at[t, tz],
                    device_id={"dp": 2 * target + tx}, device_id_type=MESH,
                )
                pl.when(target != tz)(lambda copy=copy: copy.start())
                along.append((target != tz, copy))

    for copy in back:
        copy.wait_recv()
    for i, ref in enumerate((dq_ref, dk_ref, dv_ref)):
        ref[...] = jnp.concatenate(
            [merge(land[0, i], land[1, i]), merge(land[2, i], land[3, i])], axis=1
        )

    if tail:
        owner = tz // 2 == core
        other = 2 * (me // 2) + 1 - core
        lanes = pl.multiple_of(128 * (1 - core), 128)
        hand = [
            pltpu.make_async_remote_copy(
                src_ref=fin.at[t, :, pl.ds(lanes, WIN)], dst_ref=fin.at[t, :, pl.ds(lanes, WIN)],
                send_sem=c_sem.at[0, t], recv_sem=c_sem.at[1, t],
                device_id={"seq": other}, device_id_type=MESH,
            )
            for t in range(TAPS)
        ]
        mine_lanes = pl.multiple_of(128 * core, 128)
        take = [
            pltpu.make_async_remote_copy(
                src_ref=fin.at[t, :, pl.ds(mine_lanes, WIN)],
                dst_ref=fin.at[t, :, pl.ds(mine_lanes, WIN)],
                send_sem=c_sem.at[0, t], recv_sem=c_sem.at[1, t],
                device_id={"seq": other}, device_id_type=MESH,
            )
            for t in range(TAPS)
        ]

        @pl.when(owner)
        def _():
            for t in range(TAPS):
                fin[t] = zs[tz % 2, t]
                for o in (1, 2, 3):
                    source = lax.rem(tz + o, 4)
                    pltpu.make_async_remote_copy(
                        src_ref=zo.at[0, t], dst_ref=zr.at[source, t],
                        send_sem=z_send.at[t, 0], recv_sem=z_recv.at[t, source],
                        device_id={"dp": 2 * source + tx}, device_id_type=MESH,
                    ).wait_recv()
                    fin[t] += zr[source, t].astype(F32)
                hand[t].start()
            for copy in hand:
                copy.wait_send()

        @pl.when(jnp.logical_not(owner))
        def _():
            for copy in take:
                copy.wait_recv()

        for t in range(TAPS):
            both = fin[t, :, pl.ds(mine_lanes, WIN)]
            gw_ref[t] = jnp.where(core == 0, both[:, :HEAD_DIM], both[:, WIN - HEAD_DIM :])
        for go, copy in along:
            pl.when(go)(lambda copy=copy: copy.wait_send())

    pl.when(has_next)(lambda: down.wait_send())
    pl.when(has_prev)(lambda: up.wait_send())
    for copy in first + grads + spread + stats + inner + back + crossing:
        copy.wait_send()
    for copy in across + [act_across, act_near]:
        copy.wait_send()

    @pl.when(forms)
    def _():
        for i in range(2):
            act_hop(i, partner).wait_send()


def store_kernel(*refs):
    for i in range(5):
        refs[5 + i][...] = refs[i][...]


def body(queries, key_rows, value_rows, conv_weight, output_gradient):
    rows, feats = queries.shape[1:]
    total = rows * N
    vmem = pl.BlockSpec(memory_space=pltpu.VMEM)
    shape = jax.ShapeDtypeStruct
    inside = lax.axis_size("dp") == 8
    gw_shape = (TAPS, 96, HEAD_DIM) if inside else (TAPS, 384, 384)
    tail = [
        pltpu.VMEM((TAPS, 384, 384), F32),
        pltpu.VMEM((TAPS, 384, 384), BF16),
        pltpu.VMEM((TAPS, 2, 96, 384), BF16),
        pltpu.VMEM((2, TAPS, 96, 384), F32),
        pltpu.VMEM((2, TAPS, 96, 384), BF16),
        pltpu.VMEM((4, TAPS, 96, 384), BF16),
        pltpu.VMEM((TAPS, 96, 384), F32),
        pltpu.SemaphoreType.DMA((TAPS, 2)),
        pltpu.SemaphoreType.DMA((TAPS, 2)),
        pltpu.SemaphoreType.DMA((TAPS, 2)),
        pltpu.SemaphoreType.DMA((TAPS, 4)),
        pltpu.SemaphoreType.DMA((2, TAPS)),
    ]
    outs = pl.pallas_call(
        kernel,
        out_shape=[shape((rows, feats), BF16)] * 4 + [shape(gw_shape, F32)],
        in_specs=[pl.BlockSpec(memory_space=pltpu.HBM)] * 5,
        out_specs=[vmem] * 5,
        scratch_shapes=[
            pltpu.VMEM((TAPS, feats, feats), BF16),
            pltpu.VMEM((3, total, WIN), BF16),
            pltpu.VMEM((rows + 2 * STEP, feats), BF16),
            pltpu.VMEM((rows, feats), BF16),
            pltpu.VMEM((total, WIN), BF16),
            pltpu.VMEM((total + 2 * STEP, 384), BF16),
            pltpu.VMEM((total, total), F32),
            pltpu.VMEM((total, WIN), BF16),
            pltpu.VMEM((total, WIN), F32),
            pltpu.VMEM((total, WIN), F32),
            pltpu.VMEM((N, total + 2 * STEP, WIN), BF16),
            pltpu.VMEM((2, N, 8, total), F32),
            pltpu.VMEM((3, total, WIN), BF16),
            pltpu.VMEM((N, 3, rows, WIN), BF16),
            pltpu.VMEM((3, rows, 384), BF16),
            pltpu.VMEM((rows, 384), BF16),
            pltpu.SemaphoreType.DMA((TAPS + 5,)),
            pltpu.SemaphoreType.DMA((13, N)),
            pltpu.SemaphoreType.DMA((13, N)),
        ] + (tail if inside else []),
        compiler_params=pltpu.CompilerParams(
            collective_id=0, has_side_effects=True, vmem_limit_bytes=int(62.5 * 2**20)
        ),
    )(
        queries[0], key_rows[0], value_rows[0], output_gradient[0],
        jnp.transpose(conv_weight, (1, 0, 2)),
    )
    if not inside:
        pieces = lax.all_to_all(
            outs[4].astype(BF16), "seq", split_axis=2, concat_axis=1, tiled=True,
            axis_index_groups=[[0, 1], [2, 3]],
        )
        gw = lax.psum_scatter(pieces.astype(F32), "dp", scatter_dimension=1, tiled=True)
        outs = [*outs[:4], gw]
    else:
        outs = pl.pallas_call(
            store_kernel,
            out_shape=[shape(out.shape, out.dtype) for out in outs],
            in_specs=[vmem] * 5,
            out_specs=[vmem] * 5,
            compiler_params=pltpu.CompilerParams(vmem_limit_bytes=int(62.5 * 2**20)),
        )(*outs)
    return (*(out[None] for out in outs[:4]), jnp.transpose(outs[4], (1, 0, 2)))


def solution(mesh):
    row_spec = P("dp", "seq", None)
    return jax.shard_map(
        body,
        mesh=mesh,
        in_specs=(row_spec, row_spec, row_spec, P(), row_spec),
        out_specs=(row_spec, row_spec, row_spec, row_spec, P("dp", None, "seq")),
        check_vma=False,
    )
```

```python
import functools
import math

import jax
import jax.numpy as jnp
from jax import lax
from jax.experimental import pallas as pl
from jax.experimental.pallas import tpu as pltpu
from jax.sharding import PartitionSpec as P

HEAD_DIM = 192
WIN = 256
TAPS = 3
STEP = 32
N = 4
F32 = jnp.float32
BF16 = jnp.bfloat16
MESH = pl.DeviceIdType.MESH

tanh_scale = 0.7978845608028654
cubic_term = 0.044715
norm_epsilon = 1e-06


def gelu_pair(value):
    square = value * value
    inner = tanh_scale * (value + cubic_term * value * square)
    tangent = jnp.tanh(inner)
    half = 0.5 * (1.0 + tangent)
    result = value * half
    slope = half + 0.5 * value * (1.0 - tangent * tangent) * tanh_scale * (
        1.0 + 3.0 * cubic_term * square
    )
    return (result, slope)


def window_start(head):
    return pl.multiple_of(384 * (head // 2) + 128 * (head % 2), 128)


def nt(a, b):
    return lax.dot_general(a, b, (((1,), (1,)), ((), ())), preferred_element_type=F32)


def tn(a, b):
    return lax.dot_general(a, b, (((0,), (0,)), ((), ())), preferred_element_type=F32)


def nn(a, b):
    return lax.dot_general(a, b, (((1,), (0,)), ((), ())), preferred_element_type=F32)


def merge(even, odd):
    return jnp.concatenate(
        [even[:, :128], even[:, 128:] + odd[:, :128], odd[:, 128:]], axis=1
    )


def as_row(column):
    wide = jnp.broadcast_to(column, (column.shape[0], 128))
    return wide.T[:8]


def as_column(row):
    return jnp.broadcast_to(row, (128, 128)).T


def kernel(
    q_ref, k_ref, v_ref, g_ref, w_hbm,
    conv_ref, dq_ref, dk_ref, dv_ref, gw_ref,
    w_ref, qkv, gh, ga, gab, gg, soft, att, normed, gn, act, stat, dqkv, land,
    xq, xa, w_sem, send_sem, recv_sem, *tail,
):
    me = lax.axis_index("seq")
    rows, feats = q_ref.shape
    ring = lax.axis_index("dp")
    tx, tz, core = ring % 2, ring // 2, me % 2
    total = rows * N
    inverse = 1.0 / math.sqrt(HEAD_DIM)
    half_lanes = pl.multiple_of(384 * (me // 2), 128)
    my_start = window_start(me)
    my_rows = pl.multiple_of(rows * me, rows)
    sends = []

    chip = me // 2
    partner = 2 * chip + 1 - core
    cross = 2 * (1 - chip) + core
    diagonal = 2 * (1 - chip) + 1 - core
    cross_rows = pl.ds(pl.multiple_of(rows * cross, rows), rows)
    their_rows = pl.ds(pl.multiple_of(rows * partner, rows), rows)
    their_start = window_start(partner)
    across_lanes = pl.multiple_of(384 * (1 - chip), 128)
    mine_in_block = pl.ds(pl.multiple_of(128 * core, 128), WIN)
    theirs_in_block = pl.ds(pl.multiple_of(128 * (1 - core), 128), WIN)

    def peer_of(o):
        return (None, partner, cross, diagonal)[o]

    def rdma(phase, o, src, dst, target=None):
        copy = pltpu.make_async_remote_copy(
            src_ref=src, dst_ref=dst,
            send_sem=send_sem.at[phase, o], recv_sem=recv_sem.at[phase, o],
            device_id={"seq": peer_of(o) if target is None else target}, device_id_type=MESH,
        )
        return copy

    loads = [pltpu.make_async_copy(w_hbm.at[t], w_ref.at[t], w_sem.at[t]) for t in range(TAPS)]
    grad_rows = pl.ds(pl.multiple_of(STEP + rows * me, STEP), rows)
    g_loads = [
        pltpu.make_async_copy(g_ref, gh.at[pl.ds(STEP, rows)], w_sem.at[TAPS]),
        pltpu.make_async_copy(g_ref.at[:, pl.ds(half_lanes, 384)], gg.at[grad_rows], w_sem.at[TAPS + 1]),
    ]
    own = [
        pltpu.make_async_copy(
            ref.at[:, pl.ds(my_start, WIN)], qkv.at[i, pl.ds(my_rows, rows)], w_sem.at[TAPS + 2 + i]
        )
        for i, ref in enumerate((q_ref, k_ref, v_ref))
    ]
    for load in g_loads + loads + own:
        load.start()

    barrier = pltpu.get_barrier_semaphore()
    for o in (1, 2, 3):
        pl.semaphore_signal(barrier, inc=1, device_id={"seq": peer_of(o)}, device_id_type=MESH)
    if tail:
        for other in [ring + 1 - 2 * tx] + [2 * lax.rem(tz + o, 4) + tx for o in (1, 2, 3)]:
            pl.semaphore_signal(barrier, inc=1, device_id={"dp": other}, device_id_type=MESH)
    pl.semaphore_wait(barrier, 7 if tail else 3)

    has_next, has_prev = me < N - 1, me > 0
    down = pltpu.make_async_remote_copy(
        src_ref=g_ref.at[pl.ds(rows - STEP, STEP)], dst_ref=gh.at[pl.ds(0, STEP)],
        send_sem=send_sem.at[0, 0], recv_sem=recv_sem.at[0, 0],
        device_id={"seq": lax.rem(me + 1, N)}, device_id_type=MESH,
    )
    up = pltpu.make_async_remote_copy(
        src_ref=g_ref.at[pl.ds(0, STEP)], dst_ref=gh.at[pl.ds(rows + STEP, STEP)],
        send_sem=send_sem.at[1, 0], recv_sem=recv_sem.at[1, 0],
        device_id={"seq": lax.rem(me + N - 1, N)}, device_id_type=MESH,
    )
    pl.when(has_next)(lambda: down.start())
    pl.when(has_prev)(lambda: up.start())

    across, first, grads = [], [], []
    for i, ref in enumerate((q_ref, k_ref, v_ref)):
        copy = rdma(i, 2, ref.at[:, pl.ds(across_lanes, 384)], xq.at[i])
        copy.start()
        across.append(copy)
    for i, ref in enumerate((q_ref, k_ref, v_ref)):
        copy = rdma(i, 1, ref.at[:, pl.ds(their_start, WIN)], qkv.at[i, pl.ds(my_rows, rows)])
        copy.start()
        first.append(copy)
    g_across = rdma(3, 2, g_ref.at[:, pl.ds(across_lanes, 384)], gg.at[grad_rows])
    g_across.start()
    g_near = rdma(3, 1, g_ref.at[:, pl.ds(half_lanes, 384)], gg.at[grad_rows])
    g_near.start()
    grads = [g_across, g_near]

    gg[pl.ds(0, STEP)] = jnp.zeros((STEP, 384), BF16)
    gg[pl.ds(STEP + total, STEP)] = jnp.zeros((STEP, 384), BF16)

    @pl.when(me == 0)
    def _():
        gh[pl.ds(0, STEP)] = jnp.zeros((STEP, feats), BF16)

    @pl.when(me == N - 1)
    def _():
        gh[pl.ds(rows + STEP, STEP)] = jnp.zeros((STEP, feats), BF16)

    pl.when(has_prev)(lambda: down.wait_recv())
    pl.when(has_next)(lambda: up.wait_recv())
    for load in g_loads + loads:
        load.wait()

    acc = nt(gh[pl.ds(2 * STEP, rows)], w_ref[0])
    acc += nt(gh[pl.ds(STEP, rows)], w_ref[1])
    acc += nt(gh[pl.ds(0, rows)], w_ref[2])
    ga[...] = acc.astype(BF16)
    ga_across = rdma(4, 2, ga.at[:, pl.ds(across_lanes, 384)], xa)
    ga_across.start()
    ga_near = rdma(4, 1, ga.at[:, pl.ds(their_start, WIN)], gab.at[pl.ds(my_rows, rows)])
    ga_near.start()
    spread = [ga_across, ga_near]
    gab[pl.ds(my_rows, rows)] = ga[:, pl.ds(my_start, WIN)]

    lane = lax.broadcasted_iota(jnp.int32, (rows, WIN), 1)
    low = 64 * (me % 2)
    mask32 = jnp.logical_and(lane >= low, lane < low + HEAD_DIM).astype(F32)
    mask = mask32.astype(BF16)

    for i in range(3):
        across[i].wait_recv()
        copy = rdma(i, 3, xq.at[i, :, theirs_in_block], qkv.at[i, cross_rows], partner)
        copy.start()
        first.append(copy)
    for i in range(3):
        qkv[i, cross_rows] = xq[i, :, mine_in_block]
    for load in own:
        load.wait()
    for copy in first:
        copy.wait_recv()
    for i in range(3):
        for b in range(N):
            part = pl.ds(b * rows, rows)
            qkv[i, part] = qkv[i, part] * mask

    keys, values = qkv[1], qkv[2]
    for b in range(N):
        part = pl.ds(b * rows, rows)
        scores = nt(qkv[0, part], keys)
        top = jnp.max(scores, axis=-1, keepdims=True)
        expo = jnp.exp((scores - top) * inverse)
        prob = expo * (1.0 / jnp.sum(expo, axis=-1, keepdims=True))
        soft[part] = prob
        out = nn(prob.astype(BF16), values).astype(BF16)
        att[part] = out
        wide = out.astype(F32)
        stat[0, me, :, b * rows : (b + 1) * rows] = as_row(
            jnp.sum(wide * wide, axis=-1, keepdims=True)
        )
    stats = []
    for o in (2, 3, 1):
        copy = rdma(5, o, stat.at[0, me], stat.at[0, me])
        copy.start()
        stats.append(copy)
    ga_across.wait_recv()
    ga_hop = rdma(4, 3, xa.at[:, theirs_in_block], gab.at[cross_rows], partner)
    ga_hop.start()
    gab[cross_rows] = xa[:, mine_in_block]
    g_across.wait_recv()
    g_cross = pl.ds(pl.multiple_of(STEP + rows * cross, STEP), rows)
    g_hop = rdma(3, 3, gg.at[g_cross], gg.at[g_cross], partner)
    g_hop.start()
    spread.append(ga_hop)
    grads.append(g_hop)
    ga_near.wait_recv()
    ga_hop.wait_recv()
    for copy in stats:
        copy.wait_recv()

    act[me, pl.ds(0, STEP)] = jnp.zeros((STEP, WIN), BF16)
    act[me, pl.ds(STEP + total, STEP)] = jnp.zeros((STEP, WIN), BF16)

    def factor(b):
        lanes = slice(b * rows, (b + 1) * rows)
        mean = (
            stat[0, 0, :1, lanes] + stat[0, 1, :1, lanes]
            + stat[0, 2, :1, lanes] + stat[0, 3, :1, lanes]
        ) * (1.0 / feats)
        one = as_column(lax.rsqrt(mean + norm_epsilon))
        return jnp.concatenate([one, one], axis=1)

    for b in range(N):
        part = pl.ds(b * rows, rows)
        x = att[part].astype(F32) * factor(b)
        value, slope = gelu_pair(x)
        act[me, pl.ds(STEP + b * rows, rows)] = value.astype(BF16)
        grad = gab[part].astype(F32) * slope * mask32
        normed[part] = x
        gn[part] = grad
        stat[1, me, :, b * rows : (b + 1) * rows] = as_row(
            jnp.sum(grad * x, axis=-1, keepdims=True)
        )
    inner = []
    for o in (2, 3, 1):
        copy = rdma(6, o, stat.at[1, me], stat.at[1, me])
        copy.start()
        inner.append(copy)

    inside = pl.ds(STEP, total)
    forms = core == 1 - chip
    act_across = pltpu.make_async_remote_copy(
        src_ref=act.at[me, inside], dst_ref=act.at[me, inside],
        send_sem=send_sem.at[7, 0], recv_sem=recv_sem.at[7, core],
        device_id={"seq": 2 * (1 - chip) + chip}, device_id_type=MESH,
    )
    act_across.start()
    act_near = rdma(11, 1, act.at[me], act.at[me])
    act_near.start()

    @pl.when(forms)
    def _():
        for i in range(2):
            act[2 * (1 - chip) + i, pl.ds(0, STEP)] = jnp.zeros((STEP, WIN), BF16)
            act[2 * (1 - chip) + i, pl.ds(STEP + total, STEP)] = jnp.zeros((STEP, WIN), BF16)

    for copy in (g_near, g_hop):
        copy.wait_recv()
    act_near.wait_recv()
    if tail:
        gwf, xs, xr, zs, zo, zr, fin, x_send, x_recv, z_send, z_recv, c_sem = tail

    def x_copy(t, j):
        there = pl.ds(pl.multiple_of(96 * (2 * j + 1 - tx), 96), 96)
        return pltpu.make_async_remote_copy(
            src_ref=xs.at[t, there], dst_ref=xr.at[t, j],
            send_sem=x_send.at[t, j], recv_sem=x_recv.at[t, j],
            device_id={"dp": ring + 1 - 2 * tx}, device_id_type=MESH,
        )

    def form_gradient():
        pair = 2 * core
        mine = merge(act[pair, inside], act[pair + 1, inside])
        mine = mine.T
        scale = 1.0 / math.sqrt(total * lax.axis_size("dp"))
        for t in range(TAPS):
            term = nn(mine, gg[pl.ds((2 - t) * STEP, total)]) * scale
            if not tail:
                gw_ref[t] = term
                continue
            gwf[t] = term
            xs[t] = term.astype(BF16)
            for j in range(2):
                x_copy(t, j).start()

    pl.when(jnp.logical_not(forms))(form_gradient)

    for copy in inner:
        copy.wait_recv()

    queries = qkv[0]
    for b in range(N):
        part = pl.ds(b * rows, rows)
        lanes = slice(b * rows, (b + 1) * rows)
        mean = (
            stat[1, 0, :1, lanes] + stat[1, 1, :1, lanes]
            + stat[1, 2, :1, lanes] + stat[1, 3, :1, lanes]
        ) * (1.0 / feats)
        one = as_column(mean)
        mean = jnp.concatenate([one, one], axis=1)
        grad = (factor(b) * (gn[part] - normed[part] * mean)).astype(BF16)
        att[part] = grad
        prob = soft[part]
        gs = nt(grad, values)
        row_inner = jnp.sum(gs * prob, axis=-1, keepdims=True)
        ds = (prob * (gs - row_inner) * inverse).astype(BF16)
        dqkv[0, part] = nn(ds, keys).astype(BF16)
        pieces = (tn(ds, queries[b * rows : (b + 1) * rows]), tn(prob.astype(BF16), grad))
        sums = pieces if b == 0 else (sums[0] + pieces[0], sums[1] + pieces[1])
    dqkv[1] = sums[0].astype(BF16)
    dqkv[2] = sums[1].astype(BF16)

    back = []
    for o in (2, 3, 1):
        there = pl.ds(pl.multiple_of(rows * peer_of(o), rows), rows)
        for i in range(3):
            copy = rdma(8 + i, o, dqkv.at[i, there], land.at[me, i])
            copy.start()
            back.append(copy)
    for i in range(3):
        land[me, i] = dqkv[i, pl.ds(my_rows, rows)]

    def act_hop(i, row):
        slot = 2 * (1 - chip) + i
        some = pl.ds(pl.multiple_of(rows * row, rows), rows + 2 * STEP)
        return rdma(12, i, act.at[slot, some], act.at[slot, some], partner)

    @pl.when(forms)
    def _():
        for i in range(2):
            slot = 2 * (1 - chip) + i
            pltpu.make_async_remote_copy(
                src_ref=act.at[slot, inside], dst_ref=act.at[slot, inside],
                send_sem=send_sem.at[7, 0], recv_sem=recv_sem.at[7, i],
                device_id={"seq": partner}, device_id_type=MESH,
            ).wait_recv()
            act_hop(i, partner).start()
        form_gradient()

    @pl.when(jnp.logical_not(forms))
    def _():
        for i in range(2):
            act_hop(i, me).wait_recv()

    near = pl.ds(my_rows, rows + 2 * STEP)
    nearby = jnp.concatenate(
        [merge(act[0, near], act[1, near]), merge(act[2, near], act[3, near])], axis=1
    )
    out = nn(nearby[:rows], w_ref[0])
    out += nn(nearby[STEP : STEP + rows], w_ref[1])
    out += nn(nearby[2 * STEP :], w_ref[2])
    conv_ref[...] = out.astype(BF16)

    step = tz + core * (3 - 2 * tz)
    near_block, next_block = core, 1 - core

    def z_copy(block, t, slot, goal):
        there = goal + core * (3 - 2 * goal)
        return pltpu.make_async_remote_copy(
            src_ref=zo.at[block, t], dst_ref=zr.at[slot, t],
            send_sem=z_send.at[t, block], recv_sem=z_recv.at[t, slot],
            device_id={"dp": 2 * there + tx}, device_id_type=MESH,
        )

    if tail:
        for t in range(TAPS):
            for j in range(2):
                x_copy(t, j).wait_recv()
                here = pl.ds(pl.multiple_of(96 * (2 * j + tx), 96), 96)
                block = gwf[t, here] + xr[t, j].astype(F32)
                zs[j, t] = block
                zo[j, t] = block.astype(BF16)

            @pl.when(step == 3)
            def _(t=t):
                z_copy(0, t, 0, 2).start()
                z_copy(1, t, 1, 2).start()

            @pl.when(step == 2)
            def _(t=t):
                for j in range(2):
                    z_copy(j, t, j, 2).wait_recv()
                    zo[j, t] = (zs[j, t] + zr[j, t].astype(F32)).astype(BF16)
                z_copy(near_block, t, 0, 0).start()
                z_copy(next_block, t, 0, 1).start()

            @pl.when(step == 1)
            def _(t=t):
                z_copy(near_block, t, 1, 0).start()

            @pl.when(step == 0)
            def _(t=t):
                z_copy(next_block, t, 1, 1).start()

    for copy in back:
        copy.wait_recv()
    for i, ref in enumerate((dq_ref, dk_ref, dv_ref)):
        ref[...] = jnp.concatenate(
            [merge(land[0, i], land[1, i]), merge(land[2, i], land[3, i])], axis=1
        )

    if tail:
        owner = step < 2
        other = 2 * (me // 2) + 1 - core
        lanes = pl.multiple_of(128 * (1 - core), 128)
        hand = [
            pltpu.make_async_remote_copy(
                src_ref=fin.at[t, :, pl.ds(lanes, WIN)], dst_ref=fin.at[t, :, pl.ds(lanes, WIN)],
                send_sem=c_sem.at[0, t], recv_sem=c_sem.at[1, t],
                device_id={"seq": other}, device_id_type=MESH,
            )
            for t in range(TAPS)
        ]
        mine_lanes = pl.multiple_of(128 * core, 128)
        take = [
            pltpu.make_async_remote_copy(
                src_ref=fin.at[t, :, pl.ds(mine_lanes, WIN)],
                dst_ref=fin.at[t, :, pl.ds(mine_lanes, WIN)],
                send_sem=c_sem.at[0, t], recv_sem=c_sem.at[1, t],
                device_id={"seq": other}, device_id_type=MESH,
            )
            for t in range(TAPS)
        ]

        @pl.when(owner)
        def _():
            for t in range(TAPS):
                fin[t] = zs[tz % 2, t]
                z_copy(0, t, 0, 0).wait_recv()
                fin[t] += zr[0, t].astype(F32)
                z_copy(0, t, 1, 0).wait_recv()
                fin[t] += zr[1, t].astype(F32)
                hand[t].start()
            for copy in hand:
                copy.wait_send()

        @pl.when(jnp.logical_not(owner))
        def _():
            for copy in take:
                copy.wait_recv()

        for t in range(TAPS):
            both = fin[t, :, pl.ds(mine_lanes, WIN)]
            gw_ref[t] = jnp.where(core == 0, both[:, :HEAD_DIM], both[:, WIN - HEAD_DIM :])
        for t in range(TAPS):

            @pl.when(step >= 2)
            def _(t=t):
                for j in range(2):
                    z_copy(j, t, 0, 0).wait_send()

            pl.when(step == 1)(lambda t=t: z_copy(near_block, t, 1, 0).wait_send())
            pl.when(step == 0)(lambda t=t: z_copy(next_block, t, 1, 1).wait_send())
            for j in range(2):
                x_copy(t, j).wait_send()

    pl.when(has_next)(lambda: down.wait_send())
    pl.when(has_prev)(lambda: up.wait_send())
    for copy in first + grads + spread + stats + inner + back:
        copy.wait_send()
    for copy in across + [act_across, act_near]:
        copy.wait_send()

    @pl.when(forms)
    def _():
        for i in range(2):
            act_hop(i, partner).wait_send()


def store_kernel(*refs):
    for i in range(5):
        refs[5 + i][...] = refs[i][...]


def body(queries, key_rows, value_rows, conv_weight, output_gradient):
    rows, feats = queries.shape[1:]
    total = rows * N
    vmem = pl.BlockSpec(memory_space=pltpu.VMEM)
    shape = jax.ShapeDtypeStruct
    inside = lax.axis_size("dp") == 8
    gw_shape = (TAPS, 96, HEAD_DIM) if inside else (TAPS, 384, 384)
    tail = [
        pltpu.VMEM((TAPS, 384, 384), F32),
        pltpu.VMEM((TAPS, 384, 384), BF16),
        pltpu.VMEM((TAPS, 2, 96, 384), BF16),
        pltpu.VMEM((2, TAPS, 96, 384), F32),
        pltpu.VMEM((2, TAPS, 96, 384), BF16),
        pltpu.VMEM((2, TAPS, 96, 384), BF16),
        pltpu.VMEM((TAPS, 96, 384), F32),
        pltpu.SemaphoreType.DMA((TAPS, 2)),
        pltpu.SemaphoreType.DMA((TAPS, 2)),
        pltpu.SemaphoreType.DMA((TAPS, 2)),
        pltpu.SemaphoreType.DMA((TAPS, 2)),
        pltpu.SemaphoreType.DMA((2, TAPS)),
    ]
    outs = pl.pallas_call(
        kernel,
        out_shape=[shape((rows, feats), BF16)] * 4 + [shape(gw_shape, F32)],
        in_specs=[pl.BlockSpec(memory_space=pltpu.HBM)] * 5,
        out_specs=[vmem] * 5,
        scratch_shapes=[
            pltpu.VMEM((TAPS, feats, feats), BF16),
            pltpu.VMEM((3, total, WIN), BF16),
            pltpu.VMEM((rows + 2 * STEP, feats), BF16),
            pltpu.VMEM((rows, feats), BF16),
            pltpu.VMEM((total, WIN), BF16),
            pltpu.VMEM((total + 2 * STEP, 384), BF16),
            pltpu.VMEM((total, total), F32),
            pltpu.VMEM((total, WIN), BF16),
            pltpu.VMEM((total, WIN), F32),
            pltpu.VMEM((total, WIN), F32),
            pltpu.VMEM((N, total + 2 * STEP, WIN), BF16),
            pltpu.VMEM((2, N, 8, total), F32),
            pltpu.VMEM((3, total, WIN), BF16),
            pltpu.VMEM((N, 3, rows, WIN), BF16),
            pltpu.VMEM((3, rows, 384), BF16),
            pltpu.VMEM((rows, 384), BF16),
            pltpu.SemaphoreType.DMA((TAPS + 5,)),
            pltpu.SemaphoreType.DMA((13, N)),
            pltpu.SemaphoreType.DMA((13, N)),
        ] + (tail if inside else []),
        compiler_params=pltpu.CompilerParams(
            collective_id=0, has_side_effects=True, vmem_limit_bytes=int(62.5 * 2**20)
        ),
    )(
        queries[0], key_rows[0], value_rows[0], output_gradient[0],
        jnp.transpose(conv_weight, (1, 0, 2)),
    )
    if not inside:
        pieces = lax.all_to_all(
            outs[4].astype(BF16), "seq", split_axis=2, concat_axis=1, tiled=True,
            axis_index_groups=[[0, 1], [2, 3]],
        )
        gw = lax.psum_scatter(pieces.astype(F32), "dp", scatter_dimension=1, tiled=True)
        outs = [*outs[:4], gw]
    else:
        outs = pl.pallas_call(
            store_kernel,
            out_shape=[shape(out.shape, out.dtype) for out in outs],
            in_specs=[vmem] * 5,
            out_specs=[vmem] * 5,
            compiler_params=pltpu.CompilerParams(vmem_limit_bytes=int(62.5 * 2**20)),
        )(*outs)
    return (*(out[None] for out in outs[:4]), jnp.transpose(outs[4], (1, 0, 2)))


def solution(mesh):
    row_spec = P("dp", "seq", None)
    return jax.shard_map(
        body,
        mesh=mesh,
        in_specs=(row_spec, row_spec, row_spec, P(), row_spec),
        out_specs=(row_spec, row_spec, row_spec, row_spec, P("dp", None, "seq")),
        check_vma=False,
    )
```

```python
import functools
import math

import jax
import jax.numpy as jnp
from jax import lax
from jax.experimental import pallas as pl
from jax.experimental.pallas import tpu as pltpu
from jax.sharding import PartitionSpec as P

HEAD_DIM = 192
WIN = 256
TAPS = 3
STEP = 32
N = 4
F32 = jnp.float32
BF16 = jnp.bfloat16
MESH = pl.DeviceIdType.MESH

tanh_scale = 0.7978845608028654
cubic_term = 0.044715
norm_epsilon = 1e-06


def gelu_pair(value):
    square = value * value
    inner = tanh_scale * (value + cubic_term * value * square)
    tangent = jnp.tanh(inner)
    half = 0.5 * (1.0 + tangent)
    result = value * half
    slope = half + 0.5 * value * (1.0 - tangent * tangent) * tanh_scale * (
        1.0 + 3.0 * cubic_term * square
    )
    return (result, slope)


def window_start(head):
    return pl.multiple_of(384 * (head // 2) + 128 * (head % 2), 128)


def nt(a, b):
    return lax.dot_general(a, b, (((1,), (1,)), ((), ())), preferred_element_type=F32)


def tn(a, b):
    return lax.dot_general(a, b, (((0,), (0,)), ((), ())), preferred_element_type=F32)


def nn(a, b):
    return lax.dot_general(a, b, (((1,), (0,)), ((), ())), preferred_element_type=F32)


def merge(even, odd):
    return jnp.concatenate(
        [even[:, :128], even[:, 128:] + odd[:, :128], odd[:, 128:]], axis=1
    )


def as_row(column):
    wide = jnp.broadcast_to(column, (column.shape[0], 128))
    return wide.T[:8]


def as_column(row):
    return jnp.broadcast_to(row, (128, 128)).T


def kernel(
    q_ref, k_ref, v_ref, g_ref, w_hbm,
    conv_ref, dq_ref, dk_ref, dv_ref, gw_ref,
    w_ref, qkv, gh, ga, gab, gg, soft, att, normed, gn, act, stat, dqkv, land,
    xq, xa, w_sem, send_sem, recv_sem, *tail,
):
    me = lax.axis_index("seq")
    rows, feats = q_ref.shape
    ring = lax.axis_index("dp")
    tx, tz, core = ring % 2, ring // 2, me % 2
    total = rows * N
    inverse = 1.0 / math.sqrt(HEAD_DIM)
    half_lanes = pl.multiple_of(384 * (me // 2), 128)
    my_start = window_start(me)
    my_rows = pl.multiple_of(rows * me, rows)
    sends = []

    chip = me // 2
    partner = 2 * chip + 1 - core
    cross = 2 * (1 - chip) + core
    diagonal = 2 * (1 - chip) + 1 - core
    cross_rows = pl.ds(pl.multiple_of(rows * cross, rows), rows)
    their_rows = pl.ds(pl.multiple_of(rows * partner, rows), rows)
    their_start = window_start(partner)
    across_lanes = pl.multiple_of(384 * (1 - chip), 128)
    mine_in_block = pl.ds(pl.multiple_of(128 * core, 128), WIN)
    theirs_in_block = pl.ds(pl.multiple_of(128 * (1 - core), 128), WIN)

    def peer_of(o):
        return (None, partner, cross, diagonal)[o]

    def rdma(phase, o, src, dst, target=None):
        copy = pltpu.make_async_remote_copy(
            src_ref=src, dst_ref=dst,
            send_sem=send_sem.at[phase, o], recv_sem=recv_sem.at[phase, o],
            device_id={"seq": peer_of(o) if target is None else target}, device_id_type=MESH,
        )
        return copy

    loads = [pltpu.make_async_copy(w_hbm.at[t], w_ref.at[t], w_sem.at[t]) for t in range(TAPS)]
    grad_rows = pl.ds(pl.multiple_of(STEP + rows * me, STEP), rows)
    g_loads = [
        pltpu.make_async_copy(g_ref, gh.at[pl.ds(STEP, rows)], w_sem.at[TAPS]),
        pltpu.make_async_copy(g_ref.at[:, pl.ds(half_lanes, 384)], gg.at[grad_rows], w_sem.at[TAPS + 1]),
    ]
    own = [
        pltpu.make_async_copy(
            ref.at[:, pl.ds(my_start, WIN)], qkv.at[i, pl.ds(my_rows, rows)], w_sem.at[TAPS + 2 + i]
        )
        for i, ref in enumerate((q_ref, k_ref, v_ref))
    ]
    for load in g_loads + loads + own:
        load.start()

    barrier = pltpu.get_barrier_semaphore()
    for o in (1, 2, 3):
        pl.semaphore_signal(barrier, inc=1, device_id={"seq": peer_of(o)}, device_id_type=MESH)
    if tail:
        for other in [ring + 1 - 2 * tx] + [2 * lax.rem(tz + o, 4) + tx for o in (1, 2, 3)]:
            pl.semaphore_signal(barrier, inc=1, device_id={"dp": other}, device_id_type=MESH)
    pl.semaphore_wait(barrier, 7 if tail else 3)

    has_next, has_prev = me < N - 1, me > 0
    down = pltpu.make_async_remote_copy(
        src_ref=g_ref.at[pl.ds(rows - STEP, STEP)], dst_ref=gh.at[pl.ds(0, STEP)],
        send_sem=send_sem.at[0, 0], recv_sem=recv_sem.at[0, 0],
        device_id={"seq": lax.rem(me + 1, N)}, device_id_type=MESH,
    )
    up = pltpu.make_async_remote_copy(
        src_ref=g_ref.at[pl.ds(0, STEP)], dst_ref=gh.at[pl.ds(rows + STEP, STEP)],
        send_sem=send_sem.at[1, 0], recv_sem=recv_sem.at[1, 0],
        device_id={"seq": lax.rem(me + N - 1, N)}, device_id_type=MESH,
    )
    pl.when(has_next)(lambda: down.start())
    pl.when(has_prev)(lambda: up.start())

    across, first, grads = [], [], []
    for i, ref in enumerate((q_ref, k_ref, v_ref)):
        copy = rdma(i, 2, ref.at[:, pl.ds(across_lanes, 384)], xq.at[i])
        copy.start()
        across.append(copy)
    for i, ref in enumerate((q_ref, k_ref, v_ref)):
        copy = rdma(i, 1, ref.at[:, pl.ds(their_start, WIN)], qkv.at[i, pl.ds(my_rows, rows)])
        copy.start()
        first.append(copy)
    g_across = rdma(3, 2, g_ref.at[:, pl.ds(across_lanes, 384)], gg.at[grad_rows])
    g_across.start()
    g_near = rdma(3, 1, g_ref.at[:, pl.ds(half_lanes, 384)], gg.at[grad_rows])
    g_near.start()
    grads = [g_across, g_near]

    gg[pl.ds(0, STEP)] = jnp.zeros((STEP, 384), BF16)
    gg[pl.ds(STEP + total, STEP)] = jnp.zeros((STEP, 384), BF16)

    @pl.when(me == 0)
    def _():
        gh[pl.ds(0, STEP)] = jnp.zeros((STEP, feats), BF16)

    @pl.when(me == N - 1)
    def _():
        gh[pl.ds(rows + STEP, STEP)] = jnp.zeros((STEP, feats), BF16)

    pl.when(has_prev)(lambda: down.wait_recv())
    pl.when(has_next)(lambda: up.wait_recv())
    for load in g_loads + loads:
        load.wait()

    acc = nt(gh[pl.ds(2 * STEP, rows)], w_ref[0])
    acc += nt(gh[pl.ds(STEP, rows)], w_ref[1])
    acc += nt(gh[pl.ds(0, rows)], w_ref[2])
    ga[...] = acc.astype(BF16)
    ga_across = rdma(4, 2, ga.at[:, pl.ds(across_lanes, 384)], xa)
    ga_across.start()
    ga_near = rdma(4, 1, ga.at[:, pl.ds(their_start, WIN)], gab.at[pl.ds(my_rows, rows)])
    ga_near.start()
    spread = [ga_across, ga_near]
    gab[pl.ds(my_rows, rows)] = ga[:, pl.ds(my_start, WIN)]

    lane = lax.broadcasted_iota(jnp.int32, (rows, WIN), 1)
    low = 64 * (me % 2)
    mask32 = jnp.logical_and(lane >= low, lane < low + HEAD_DIM).astype(F32)
    mask = mask32.astype(BF16)

    def arrive(i):
        across[i].wait_recv()
        copy = rdma(i, 3, xq.at[i, :, theirs_in_block], qkv.at[i, cross_rows], partner)
        copy.start()
        first.append(copy)
        qkv[i, cross_rows] = xq[i, :, mine_in_block]
        return copy

    def settle(i, hop):
        own[i].wait()
        first[i].wait_recv()
        hop.wait_recv()
        for b in range(N):
            part = pl.ds(b * rows, rows)
            qkv[i, part] = qkv[i, part] * mask

    hops = [arrive(0), arrive(1)]
    settle(0, hops[0])
    settle(1, hops[1])
    keys = qkv[1]
    for b in range(N):
        part = pl.ds(b * rows, rows)
        scores = nt(qkv[0, part], keys)
        top = jnp.max(scores, axis=-1, keepdims=True)
        expo = jnp.exp((scores - top) * inverse)
        soft[part] = expo * (1.0 / jnp.sum(expo, axis=-1, keepdims=True))
        if b == 1:
            hops.append(arrive(2))
    settle(2, hops[2])
    values = qkv[2]
    for b in range(N):
        part = pl.ds(b * rows, rows)
        out = nn(soft[part].astype(BF16), values).astype(BF16)
        att[part] = out
        wide = out.astype(F32)
        stat[0, me, :, b * rows : (b + 1) * rows] = as_row(
            jnp.sum(wide * wide, axis=-1, keepdims=True)
        )
    stats = []
    for o in (2, 3, 1):
        copy = rdma(5, o, stat.at[0, me], stat.at[0, me])
        copy.start()
        stats.append(copy)
    ga_across.wait_recv()
    ga_hop = rdma(4, 3, xa.at[:, theirs_in_block], gab.at[cross_rows], partner)
    ga_hop.start()
    gab[cross_rows] = xa[:, mine_in_block]
    g_across.wait_recv()
    g_cross = pl.ds(pl.multiple_of(STEP + rows * cross, STEP), rows)
    g_hop = rdma(3, 3, gg.at[g_cross], gg.at[g_cross], partner)
    g_hop.start()
    spread.append(ga_hop)
    grads.append(g_hop)
    ga_near.wait_recv()
    ga_hop.wait_recv()
    for copy in stats:
        copy.wait_recv()

    act[me, pl.ds(0, STEP)] = jnp.zeros((STEP, WIN), BF16)
    act[me, pl.ds(STEP + total, STEP)] = jnp.zeros((STEP, WIN), BF16)

    def factor(b):
        lanes = slice(b * rows, (b + 1) * rows)
        mean = (
            stat[0, 0, :1, lanes] + stat[0, 1, :1, lanes]
            + stat[0, 2, :1, lanes] + stat[0, 3, :1, lanes]
        ) * (1.0 / feats)
        one = as_column(lax.rsqrt(mean + norm_epsilon))
        return jnp.concatenate([one, one], axis=1)

    for b in range(N):
        part = pl.ds(b * rows, rows)
        x = att[part].astype(F32) * factor(b)
        value, slope = gelu_pair(x)
        act[me, pl.ds(STEP + b * rows, rows)] = value.astype(BF16)
        grad = gab[part].astype(F32) * slope * mask32
        normed[part] = x
        gn[part] = grad
        stat[1, me, :, b * rows : (b + 1) * rows] = as_row(
            jnp.sum(grad * x, axis=-1, keepdims=True)
        )
    inner = []
    for o in (2, 3, 1):
        copy = rdma(6, o, stat.at[1, me], stat.at[1, me])
        copy.start()
        inner.append(copy)

    inside = pl.ds(STEP, total)
    forms = core == 1 - chip
    act_across = pltpu.make_async_remote_copy(
        src_ref=act.at[me, inside], dst_ref=act.at[me, inside],
        send_sem=send_sem.at[7, 0], recv_sem=recv_sem.at[7, core],
        device_id={"seq": 2 * (1 - chip) + chip}, device_id_type=MESH,
    )
    act_across.start()
    act_near = rdma(11, 1, act.at[me], act.at[me])
    act_near.start()

    @pl.when(forms)
    def _():
        for i in range(2):
            act[2 * (1 - chip) + i, pl.ds(0, STEP)] = jnp.zeros((STEP, WIN), BF16)
            act[2 * (1 - chip) + i, pl.ds(STEP + total, STEP)] = jnp.zeros((STEP, WIN), BF16)

    for copy in (g_near, g_hop):
        copy.wait_recv()
    act_near.wait_recv()
    if tail:
        gwf, xs, xr, zs, zo, zr, fin, x_send, x_recv, z_send, z_recv, c_sem = tail

    def x_copy(t, j):
        there = pl.ds(pl.multiple_of(96 * (2 * j + 1 - tx), 96), 96)
        return pltpu.make_async_remote_copy(
            src_ref=xs.at[t, there], dst_ref=xr.at[t, j],
            send_sem=x_send.at[t, j], recv_sem=x_recv.at[t, j],
            device_id={"dp": ring + 1 - 2 * tx}, device_id_type=MESH,
        )

    def form_gradient():
        pair = 2 * core
        mine = merge(act[pair, inside], act[pair + 1, inside])
        mine = mine.T
        scale = 1.0 / math.sqrt(total * lax.axis_size("dp"))
        for t in range(TAPS):
            term = nn(mine, gg[pl.ds((2 - t) * STEP, total)]) * scale
            if not tail:
                gw_ref[t] = term
                continue
            gwf[t] = term
            xs[t] = term.astype(BF16)
            for j in range(2):
                x_copy(t, j).start()

    pl.when(jnp.logical_not(forms))(form_gradient)

    for copy in inner:
        copy.wait_recv()

    queries = qkv[0]
    for b in range(N):
        part = pl.ds(b * rows, rows)
        lanes = slice(b * rows, (b + 1) * rows)
        mean = (
            stat[1, 0, :1, lanes] + stat[1, 1, :1, lanes]
            + stat[1, 2, :1, lanes] + stat[1, 3, :1, lanes]
        ) * (1.0 / feats)
        one = as_column(mean)
        mean = jnp.concatenate([one, one], axis=1)
        grad = (factor(b) * (gn[part] - normed[part] * mean)).astype(BF16)
        att[part] = grad
        prob = soft[part]
        gs = nt(grad, values)
        row_inner = jnp.sum(gs * prob, axis=-1, keepdims=True)
        ds = (prob * (gs - row_inner) * inverse).astype(BF16)
        dqkv[0, part] = nn(ds, keys).astype(BF16)
        pieces = (tn(ds, queries[b * rows : (b + 1) * rows]), tn(prob.astype(BF16), grad))
        sums = pieces if b == 0 else (sums[0] + pieces[0], sums[1] + pieces[1])
    dqkv[1] = sums[0].astype(BF16)
    dqkv[2] = sums[1].astype(BF16)

    back = []
    for o in (2, 3, 1):
        there = pl.ds(pl.multiple_of(rows * peer_of(o), rows), rows)
        for i in range(3):
            copy = rdma(8 + i, o, dqkv.at[i, there], land.at[me, i])
            copy.start()
            back.append(copy)
    for i in range(3):
        land[me, i] = dqkv[i, pl.ds(my_rows, rows)]

    def act_hop(i, row):
        slot = 2 * (1 - chip) + i
        some = pl.ds(pl.multiple_of(rows * row, rows), rows + 2 * STEP)
        return rdma(12, i, act.at[slot, some], act.at[slot, some], partner)

    @pl.when(forms)
    def _():
        for i in range(2):
            slot = 2 * (1 - chip) + i
            pltpu.make_async_remote_copy(
                src_ref=act.at[slot, inside], dst_ref=act.at[slot, inside],
                send_sem=send_sem.at[7, 0], recv_sem=recv_sem.at[7, i],
                device_id={"seq": partner}, device_id_type=MESH,
            ).wait_recv()
            act_hop(i, partner).start()
        form_gradient()

    step = tz + core * (3 - 2 * tz)
    near_block, next_block = core, 1 - core

    def z_copy(block, t, slot, goal):
        there = goal + core * (3 - 2 * goal)
        return pltpu.make_async_remote_copy(
            src_ref=zo.at[block, t], dst_ref=zr.at[slot, t],
            send_sem=z_send.at[t, block], recv_sem=z_recv.at[t, slot],
            device_id={"dp": 2 * there + tx}, device_id_type=MESH,
        )

    if tail:
        for t in range(TAPS):
            for j in range(2):
                x_copy(t, j).wait_recv()
                here = pl.ds(pl.multiple_of(96 * (2 * j + tx), 96), 96)
                block = gwf[t, here] + xr[t, j].astype(F32)
                zs[j, t] = block
                zo[j, t] = block.astype(BF16)

            @pl.when(step == 3)
            def _(t=t):
                z_copy(0, t, 0, 2).start()
                z_copy(1, t, 1, 2).start()

            @pl.when(step == 2)
            def _(t=t):
                for j in range(2):
                    z_copy(j, t, j, 2).wait_recv()
                    zo[j, t] = (zs[j, t] + zr[j, t].astype(F32)).astype(BF16)
                z_copy(near_block, t, 0, 0).start()
                z_copy(next_block, t, 0, 1).start()

            @pl.when(step == 1)
            def _(t=t):
                z_copy(near_block, t, 1, 0).start()

            @pl.when(step == 0)
            def _(t=t):
                z_copy(next_block, t, 1, 1).start()

    @pl.when(jnp.logical_not(forms))
    def _():
        for i in range(2):
            act_hop(i, me).wait_recv()

    near = pl.ds(my_rows, rows + 2 * STEP)
    nearby = jnp.concatenate(
        [merge(act[0, near], act[1, near]), merge(act[2, near], act[3, near])], axis=1
    )
    out = nn(nearby[:rows], w_ref[0])
    out += nn(nearby[STEP : STEP + rows], w_ref[1])
    out += nn(nearby[2 * STEP :], w_ref[2])
    conv_ref[...] = out.astype(BF16)

    for copy in back:
        copy.wait_recv()
    for i, ref in enumerate((dq_ref, dk_ref, dv_ref)):
        ref[...] = jnp.concatenate(
            [merge(land[0, i], land[1, i]), merge(land[2, i], land[3, i])], axis=1
        )

    if tail:
        owner = step < 2
        other = 2 * (me // 2) + 1 - core
        lanes = pl.multiple_of(128 * (1 - core), 128)
        hand = [
            pltpu.make_async_remote_copy(
                src_ref=fin.at[t, :, pl.ds(lanes, WIN)], dst_ref=fin.at[t, :, pl.ds(lanes, WIN)],
                send_sem=c_sem.at[0, t], recv_sem=c_sem.at[1, t],
                device_id={"seq": other}, device_id_type=MESH,
            )
            for t in range(TAPS)
        ]
        mine_lanes = pl.multiple_of(128 * core, 128)
        take = [
            pltpu.make_async_remote_copy(
                src_ref=fin.at[t, :, pl.ds(mine_lanes, WIN)],
                dst_ref=fin.at[t, :, pl.ds(mine_lanes, WIN)],
                send_sem=c_sem.at[0, t], recv_sem=c_sem.at[1, t],
                device_id={"seq": other}, device_id_type=MESH,
            )
            for t in range(TAPS)
        ]

        @pl.when(owner)
        def _():
            for t in range(TAPS):
                fin[t] = zs[tz % 2, t]
                z_copy(0, t, 0, 0).wait_recv()
                fin[t] += zr[0, t].astype(F32)
                z_copy(0, t, 1, 0).wait_recv()
                fin[t] += zr[1, t].astype(F32)
                hand[t].start()
            for copy in hand:
                copy.wait_send()

        @pl.when(jnp.logical_not(owner))
        def _():
            for copy in take:
                copy.wait_recv()

        for t in range(TAPS):
            both = fin[t, :, pl.ds(mine_lanes, WIN)]
            gw_ref[t] = jnp.where(core == 0, both[:, :HEAD_DIM], both[:, WIN - HEAD_DIM :])
        for t in range(TAPS):

            @pl.when(step >= 2)
            def _(t=t):
                for j in range(2):
                    z_copy(j, t, 0, 0).wait_send()

            pl.when(step == 1)(lambda t=t: z_copy(near_block, t, 1, 0).wait_send())
            pl.when(step == 0)(lambda t=t: z_copy(next_block, t, 1, 1).wait_send())
            for j in range(2):
                x_copy(t, j).wait_send()

    pl.when(has_next)(lambda: down.wait_send())
    pl.when(has_prev)(lambda: up.wait_send())
    for copy in first + grads + spread + stats + inner + back:
        copy.wait_send()
    for copy in across + [act_across, act_near]:
        copy.wait_send()

    @pl.when(forms)
    def _():
        for i in range(2):
            act_hop(i, partner).wait_send()


def store_kernel(*refs):
    for i in range(5):
        refs[5 + i][...] = refs[i][...]


def body(queries, key_rows, value_rows, conv_weight, output_gradient):
    rows, feats = queries.shape[1:]
    total = rows * N
    vmem = pl.BlockSpec(memory_space=pltpu.VMEM)
    shape = jax.ShapeDtypeStruct
    inside = lax.axis_size("dp") == 8
    gw_shape = (TAPS, 96, HEAD_DIM) if inside else (TAPS, 384, 384)
    tail = [
        pltpu.VMEM((TAPS, 384, 384), F32),
        pltpu.VMEM((TAPS, 384, 384), BF16),
        pltpu.VMEM((TAPS, 2, 96, 384), BF16),
        pltpu.VMEM((2, TAPS, 96, 384), F32),
        pltpu.VMEM((2, TAPS, 96, 384), BF16),
        pltpu.VMEM((2, TAPS, 96, 384), BF16),
        pltpu.VMEM((TAPS, 96, 384), F32),
        pltpu.SemaphoreType.DMA((TAPS, 2)),
        pltpu.SemaphoreType.DMA((TAPS, 2)),
        pltpu.SemaphoreType.DMA((TAPS, 2)),
        pltpu.SemaphoreType.DMA((TAPS, 2)),
        pltpu.SemaphoreType.DMA((2, TAPS)),
    ]
    outs = pl.pallas_call(
        kernel,
        out_shape=[shape((rows, feats), BF16)] * 4 + [shape(gw_shape, F32)],
        in_specs=[pl.BlockSpec(memory_space=pltpu.HBM)] * 5,
        out_specs=[vmem] * 5,
        scratch_shapes=[
            pltpu.VMEM((TAPS, feats, feats), BF16),
            pltpu.VMEM((3, total, WIN), BF16),
            pltpu.VMEM((rows + 2 * STEP, feats), BF16),
            pltpu.VMEM((rows, feats), BF16),
            pltpu.VMEM((total, WIN), BF16),
            pltpu.VMEM((total + 2 * STEP, 384), BF16),
            pltpu.VMEM((total, total), F32),
            pltpu.VMEM((total, WIN), BF16),
            pltpu.VMEM((total, WIN), F32),
            pltpu.VMEM((total, WIN), F32),
            pltpu.VMEM((N, total + 2 * STEP, WIN), BF16),
            pltpu.VMEM((2, N, 8, total), F32),
            pltpu.VMEM((3, total, WIN), BF16),
            pltpu.VMEM((N, 3, rows, WIN), BF16),
            pltpu.VMEM((3, rows, 384), BF16),
            pltpu.VMEM((rows, 384), BF16),
            pltpu.SemaphoreType.DMA((TAPS + 5,)),
            pltpu.SemaphoreType.DMA((13, N)),
            pltpu.SemaphoreType.DMA((13, N)),
        ] + (tail if inside else []),
        compiler_params=pltpu.CompilerParams(
            collective_id=0, has_side_effects=True, vmem_limit_bytes=int(62.5 * 2**20)
        ),
    )(
        queries[0], key_rows[0], value_rows[0], output_gradient[0],
        jnp.transpose(conv_weight, (1, 0, 2)),
    )
    if not inside:
        pieces = lax.all_to_all(
            outs[4].astype(BF16), "seq", split_axis=2, concat_axis=1, tiled=True,
            axis_index_groups=[[0, 1], [2, 3]],
        )
        gw = lax.psum_scatter(pieces.astype(F32), "dp", scatter_dimension=1, tiled=True)
        outs = [*outs[:4], gw]
    else:
        outs = pl.pallas_call(
            store_kernel,
            out_shape=[shape(out.shape, out.dtype) for out in outs],
            in_specs=[vmem] * 5,
            out_specs=[vmem] * 5,
            compiler_params=pltpu.CompilerParams(vmem_limit_bytes=int(62.5 * 2**20)),
        )(*outs)
    return (*(out[None] for out in outs[:4]), jnp.transpose(outs[4], (1, 0, 2)))


def solution(mesh):
    row_spec = P("dp", "seq", None)
    return jax.shard_map(
        body,
        mesh=mesh,
        in_specs=(row_spec, row_spec, row_spec, P(), row_spec),
        out_specs=(row_spec, row_spec, row_spec, row_spec, P("dp", None, "seq")),
        check_vma=False,
    )
```
